512 devices in a mesh: seq: 64 (over y, z), head: 8 (over x, core).
Axes of the slice: x: 4, y: 4, z: 16, core: 2. Of those that a mesh axis runs over, the one named last changes fastest.
Arguments:
- queries: bfloat16 [65536, 2048], P('seq', 'head'), may hold values from -140 to 140
- context_grad: bfloat16 [65536, 2048], P('seq', 'head'), may hold values from -6 to 6
- database: bfloat16 [1024, 128, 1024], P('seq'), may hold values from -6 to 6
- neighbour_ids: int32 [1024, 2], P('seq'), may hold values from 0 to 1023, as said below
- owner_map: int32 [1024], replicated, may hold values from 0 to 1023, as said below
- key_weight: bfloat16 [1024, 2048], P('seq', 'head'), may hold values from -0.1875 to 0.1875
- value_weight: bfloat16 [1024, 2048], P('seq', 'head'), may hold values from -0.1875 to 0.1875
Outputs:
- context: bfloat16 [65536, 2048], P('seq', 'head')
- query_grad: bfloat16 [65536, 2048], P('seq', 'head')
The draws below stay inside these ranges and needn't reach their ends.
Inputs may be any that keep to these rules, and one draw needn't show every extreme that they name: A permutation: row id r is stored at position owner_map[r] of database, on index owner_map[r] // 16 of seq. `neighbour_ids`: through owner_map, the 32 neighbours named by the rows of one index of seq are stored at most 1 on any one index of seq; in every draw one index of seq stores exactly 1 of them for every index of seq.
All inputs are finite; a program needn't handle non-finite values.
Results may differ from the reference program's by a relative error of at most 0.015.
The reference program's roundings to bfloat16 on the way (of `shifted_queries`, `shifted_grads`, `neighbour_keys`, `neighbour_values`, `probs_low`, `shifted_context`, `dscore` and `shifted_qgrad`) count: a program that leaves them out, or rounds other values in their place, can miss the bound.
Values may be sent and summed in bfloat16 or wider, within the bound.
No kernel may reach another device: no remote copies, remote signals or barrier semaphores. Data moves between devices by JAX's collectives and lax.ppermute only.
A program may use at most 64 MiB of HBM per device.

```python
import jax
import jax.numpy as jnp
from jax import lax

HEADS = 16
DH = 128
ENC = 1024
BLOCK = 64
NBR = 2
DB_DEV = 16
NEIGH_LEN = 128
HD = 2048
BLOCK_DEV = 16
TOKENS = 65536
BLOCKS = 1024
DB_ROWS = 1024
CAP = 1
N_SEQ = 64


def placement_table(key):
    return jax.random.permutation(jax.random.fold_in(key, 101), DB_ROWS).astype(jnp.int32)


def draw_queries(key, part):
    key = jax.random.fold_in(key, 7)
    base_key = jax.random.fold_in(key, 0)
    base_values = jax.random.truncated_normal(base_key, -6.0, 6.0, (TOKENS, HD), jnp.float32)
    return base_values.astype(jnp.bfloat16)


def draw_owner_map(key, part):
    return placement_table(key)


def draw_neighbour_ids(key, part):
    placement = placement_table(key)
    key = jax.random.fold_in(key, 11)
    hot_key, order_key, shuffle_key, row_key = jax.random.split(key, 4)
    slot_total = N_SEQ * CAP
    ask_total = NBR * BLOCK_DEV
    hot_owner = jax.random.randint(hot_key, (), 0, N_SEQ)
    labels = jnp.arange(slot_total, dtype=jnp.int32)

    def one_device(device):
        scramble = jax.random.permutation(jax.random.fold_in(order_key, device), slot_total).astype(jnp.int32)
        priority = jnp.where(labels // CAP == hot_owner, 0, slot_total) + scramble
        chosen = jnp.argsort(priority)[:ask_total].astype(jnp.int32)
        mixing = jax.random.permutation(jax.random.fold_in(shuffle_key, device), ask_total)
        return chosen[mixing] // CAP
    owners = jax.vmap(one_device)(jnp.arange(N_SEQ, dtype=jnp.int32))
    local_row = jax.random.randint(row_key, (N_SEQ, ask_total), 0, DB_DEV)
    stored = owners * DB_DEV + local_row
    inverse = jnp.argsort(placement).astype(jnp.int32)
    return inverse[stored].reshape(BLOCKS, NBR).astype(jnp.int32)


def shard_levels(stream_key, dims, cuts, least, top_value):
    level = 1.0
    for axis_at, shards_of in cuts:
        heights = jax.random.uniform(jax.random.fold_in(jax.random.fold_in(stream_key, 6), axis_at), (shards_of,), jnp.float32, least / len(cuts), top_value / len(cuts))
        level = level * jnp.repeat(jnp.exp(heights), dims[axis_at] // shards_of).reshape((-1,) + (1,) * (len(dims) - 1 - axis_at))
    return level


def scatter_about(own_key, extent, scale, reach, shards=(), held_as=jnp.bfloat16):
    drawn = scale * jax.random.normal(own_key, extent, jnp.float32)
    if shards:
        drawn = drawn * shard_levels(own_key, extent, shards, -0.22, 0.18)
    return jnp.clip(drawn, -reach, reach).astype(held_as)


def setup_inputs(seed: int = 0) -> dict:
    key_list = jax.random.split(jax.random.key(seed), 8)
    queries = draw_queries(jax.random.fold_in(key_list[7], 71), 0)
    context_grad = scatter_about(key_list[1], (TOKENS, HD), 1.0, 6.0, ((0, 64), (1, 8)))
    database = scatter_about(key_list[2], (DB_ROWS, NEIGH_LEN, ENC), 1.0, 6.0, ((0, 64),))
    neighbour_ids = draw_neighbour_ids(jax.random.fold_in(key_list[7], 71), 0)
    owner_map = draw_owner_map(jax.random.fold_in(key_list[7], 71), 0)
    key_weight = scatter_about(key_list[5], (ENC, HD), ENC ** -0.5, 0.1875, ((0, 64), (1, 8)))
    value_weight = scatter_about(key_list[6], (ENC, HD), ENC ** -0.5, 0.1875, ((0, 64), (1, 8)))
    return dict(queries=queries, context_grad=context_grad, database=database, neighbour_ids=neighbour_ids, owner_map=owner_map, key_weight=key_weight, value_weight=value_weight)


def attend_block(shifted_queries, shifted_grads, keys_block, values_block):
    score_scale = DH ** -0.5
    query_f = shifted_queries.astype(jnp.float32)
    grad_f = shifted_grads.astype(jnp.float32)
    keys_f = keys_block.astype(jnp.float32)
    values_f = values_block.astype(jnp.float32)
    scores = jnp.einsum("cqhd,ckhd->chqk", query_f, keys_f) * score_scale
    row_max = jnp.max(scores, axis=-1, keepdims=True)
    weights = jnp.exp(scores - row_max)
    probabilities = weights / jnp.sum(weights, axis=-1, keepdims=True)
    probs_low = probabilities.astype(jnp.bfloat16)
    shifted_context = jnp.einsum("chqk,ckhd->cqhd", probs_low.astype(jnp.float32), values_f).astype(jnp.bfloat16)
    prob_grad = jnp.einsum("cqhd,ckhd->chqk", grad_f, values_f)
    row_delta = jnp.sum(probabilities * prob_grad, axis=-1, keepdims=True)
    dscore = (probabilities * (prob_grad - row_delta) * score_scale).astype(jnp.bfloat16)
    shifted_qgrad = jnp.einsum("chqk,ckhd->cqhd", dscore.astype(jnp.float32), keys_f).astype(jnp.bfloat16)
    return shifted_context, shifted_qgrad


def reference(queries, context_grad, database, neighbour_ids, owner_map, key_weight, value_weight):
    margin = BLOCK - 1
    padding = jnp.zeros((margin, HD), jnp.bfloat16)
    shifted_queries = jnp.concatenate([queries[margin:], padding], axis=0)
    shifted_grads = jnp.concatenate([context_grad[margin:], padding], axis=0)
    shifted_queries = shifted_queries.reshape(N_SEQ, BLOCK_DEV, BLOCK, HEADS, DH)
    shifted_grads = shifted_grads.reshape(N_SEQ, BLOCK_DEV, BLOCK, HEADS, DH)
    flat_rows = database.reshape(DB_ROWS * NEIGH_LEN, ENC)
    neighbour_keys = jnp.dot(flat_rows, key_weight, preferred_element_type=jnp.float32).astype(jnp.bfloat16)
    neighbour_values = jnp.dot(flat_rows, value_weight, preferred_element_type=jnp.float32).astype(jnp.bfloat16)
    neighbour_keys = neighbour_keys.reshape(DB_ROWS, NEIGH_LEN, HEADS, DH)
    neighbour_values = neighbour_values.reshape(DB_ROWS, NEIGH_LEN, HEADS, DH)
    stored = owner_map[neighbour_ids].astype(jnp.int32).reshape(N_SEQ, BLOCK_DEV * NBR)

    def one_group(operands):
        query_group, grad_group, rows_group = operands
        keys_block = neighbour_keys[rows_group].reshape(BLOCK_DEV, NBR * NEIGH_LEN, HEADS, DH)
        values_block = neighbour_values[rows_group].reshape(BLOCK_DEV, NBR * NEIGH_LEN, HEADS, DH)
        return attend_block(query_group, grad_group, keys_block, values_block)

    shifted_context, shifted_qgrad = lax.map(one_group, (shifted_queries, shifted_grads, stored))
    shifted_context = shifted_context.reshape(TOKENS, HD)
    shifted_qgrad = shifted_qgrad.reshape(TOKENS, HD)
    context = jnp.concatenate([padding, shifted_context[:TOKENS - margin]], axis=0)
    query_grad = jnp.concatenate([padding, shifted_qgrad[:TOKENS - margin]], axis=0)
    return context, query_grad
```

```python
import jax
import jax.numpy as jnp
from jax import lax
from jax.experimental import pallas as pl
from jax.experimental.pallas import tpu as pltpu
from jax.sharding import PartitionSpec as P

DH = 128
BLOCK = 64
Z = 16
PIECES = (512, 512)
GROUP = 4


def shifted(value, axis, steps):
    count = lax.axis_size(axis)
    first, last = (max(0, -steps), min(count, count - steps))
    return lax.ppermute(value, axis, [(source, source + steps) for source in range(first, last)])


def attend(query, grad, key, value):
    scale = DH ** (-0.5)
    last = (((1,), (1,)), ((), ()))
    scores = lax.dot_general(query, key, last, preferred_element_type=jnp.float32) * scale
    prob_grad = lax.dot_general(grad, value, last, preferred_element_type=jnp.float32)
    weights = jnp.exp(scores - jnp.max(scores, axis=-1, keepdims=True))
    probabilities = weights / jnp.sum(weights, axis=-1, keepdims=True)
    context = jnp.dot(
        probabilities.astype(jnp.bfloat16), value, preferred_element_type=jnp.float32
    )
    delta = jnp.sum(probabilities * prob_grad, axis=-1, keepdims=True)
    dscore = (probabilities * (prob_grad - delta) * scale).astype(jnp.bfloat16)
    qgrad = jnp.dot(dscore, key, preferred_element_type=jnp.float32)
    return context, qgrad


def project(piece_refs, weight_ref, kv_ref):
    total = None
    start = 0
    for piece_ref in piece_refs:
        width = piece_ref.shape[-1]
        rows = piece_ref[...].reshape(-1, width)
        term = jnp.dot(
            rows, weight_ref[start : start + width, :], preferred_element_type=jnp.float32
        )
        total = term if total is None else total + term
        start += width
    kv_ref[...] = total.astype(jnp.bfloat16).reshape(kv_ref.shape)


def attend_block(at, query_ref, grad_ref, kv_ref):
    width = query_ref.shape[1]
    rows = pl.ds(at * BLOCK, BLOCK)
    contexts, qgrads = [], []
    for head in range(width // DH):
        own = slice(head * DH, (head + 1) * DH)
        theirs = slice(width + head * DH, width + (head + 1) * DH)
        key = kv_ref[:, at, :, own].reshape(-1, DH)
        value = kv_ref[:, at, :, theirs].reshape(-1, DH)
        context, qgrad = attend(query_ref[rows, own], grad_ref[rows, own], key, value)
        contexts.append(pltpu.roll(context, BLOCK - 1, 0))
        qgrads.append(pltpu.roll(qgrad, BLOCK - 1, 0))
    return jnp.concatenate(contexts, axis=1), jnp.concatenate(qgrads, axis=1)


def halo_kernel(query_ref, grad_ref, *refs):
    *piece_refs, weight_ref, halo_ref, kv_ref = refs
    project(piece_refs, weight_ref, kv_ref)
    context, qgrad = attend_block(0, query_ref, grad_ref, kv_ref)
    halo_ref[:BLOCK, :] = context.astype(jnp.bfloat16)
    halo_ref[BLOCK:, :] = qgrad.astype(jnp.bfloat16)


def main_kernel(query_ref, grad_ref, *refs):
    *piece_refs, weight_ref, context_ref, qgrad_ref, kv_ref, carry_ref = refs

    @pl.when(pl.program_id(0) == 0)
    def _():
        carry_ref[...] = jnp.zeros_like(carry_ref)

    project(piece_refs, weight_ref, kv_ref)
    row = lax.broadcasted_iota(jnp.int32, (BLOCK, query_ref.shape[1]), 0)
    before = carry_ref[0], carry_ref[1]
    for at in range(kv_ref.shape[1]):
        now = attend_block(at, query_ref, grad_ref, kv_ref)
        for out_ref, old, new in zip((context_ref, qgrad_ref), before, now):
            tile = jnp.where(row < BLOCK - 1, old, new)
            out_ref[at * BLOCK : (at + 1) * BLOCK, :] = tile.astype(jnp.bfloat16)
        before = now
    carry_ref[0], carry_ref[1] = before


def first_rows_kernel(halo_ref, context_ref, qgrad_ref, context_out, qgrad_out):
    row = lax.broadcasted_iota(jnp.int32, context_ref.shape, 0)
    for at, (old, out) in enumerate(((context_ref, context_out), (qgrad_ref, qgrad_out))):
        new = halo_ref[at * BLOCK : (at + 1) * BLOCK, :].astype(jnp.float32)
        tile = jnp.where(row < BLOCK - 1, new, old[...].astype(jnp.float32))
        out[...] = tile.astype(jnp.bfloat16)


def attention(shifted_queries, shifted_grads, pieces, weight):
    tokens, width = shifted_queries.shape
    parts, blocks, part_tokens, _ = pieces[0].shape
    enc_width = weight.shape[0]
    params = pltpu.CompilerParams(vmem_limit_bytes=48 * 1024 * 1024)

    def operands(group, first):
        place = pl.BlockSpec((group * BLOCK, width), lambda i: (i + first, 0))
        return [place, place] + [
            pl.BlockSpec((parts, group, part_tokens, p.shape[-1]), lambda i: (0, i + first, 0, 0))
            for p in pieces
        ] + [pl.BlockSpec((enc_width, 2 * width), lambda i: (0, 0))]

    def cost(count):
        keys = parts * part_tokens
        return pl.CostEstimate(
            flops=count * 2 * keys * 2 * width * (enc_width + 2 * BLOCK),
            bytes_accessed=count * 2 * (keys * enc_width + 4 * BLOCK * width)
            + 4 * enc_width * width,
            transcendentals=count * keys * BLOCK * width // DH,
        )

    def kv_scratch(group):
        return pltpu.VMEM((parts, group, part_tokens, 2 * width), jnp.bfloat16)

    inputs = (shifted_queries, shifted_grads, *pieces, weight)
    halo = pl.pallas_call(
        halo_kernel,
        grid=(1,),
        out_shape=jax.ShapeDtypeStruct((2 * BLOCK, width), jnp.bfloat16),
        in_specs=operands(1, blocks - 1),
        out_specs=pl.BlockSpec((2 * BLOCK, width), lambda i: (0, 0)),
        scratch_shapes=[kv_scratch(1)],
        compiler_params=params,
        cost_estimate=cost(1),
        name="last_block",
    )(*inputs)
    halo = shifted(halo, "seq", 1)
    out = jax.ShapeDtypeStruct((tokens, width), jnp.bfloat16)
    place = pl.BlockSpec((GROUP * BLOCK, width), lambda i: (i, 0))
    context, query_grad = pl.pallas_call(
        main_kernel,
        grid=(blocks // GROUP,),
        out_shape=(out, out),
        in_specs=operands(GROUP, 0),
        out_specs=(place, place),
        scratch_shapes=[kv_scratch(GROUP), pltpu.VMEM((2, BLOCK, width), jnp.float32)],
        compiler_params=params,
        cost_estimate=cost(blocks),
        name="blocks",
    )(*inputs)
    place = pl.BlockSpec((BLOCK, width), lambda i: (0, 0))
    return pl.pallas_call(
        first_rows_kernel,
        grid=(1,),
        out_shape=(out, out),
        in_specs=[pl.BlockSpec((2 * BLOCK, width), lambda i: (0, 0)), place, place],
        out_specs=(place, place),
        input_output_aliases={1: 0, 2: 1},
        name="first_rows",
    )(halo, context, query_grad)


def body(queries, context_grad, database, neighbour_ids, owner_map, key_weight, value_weight):
    margin = BLOCK - 1
    seq_count = lax.axis_size("seq")
    head_devices = lax.axis_size("head")
    y_count = seq_count // Z
    local_rows, neigh_tokens, enc_width = database.shape
    part_tokens = neigh_tokens // head_devices
    my_head = lax.axis_index("head")

    request_ids = neighbour_ids.reshape(-1)
    row_labels = jnp.arange(owner_map.shape[0], dtype=jnp.int32)
    stored = jnp.sum(
        jnp.where(request_ids[:, None] == row_labels[None, :], owner_map[None, :], 0),
        axis=1,
        dtype=jnp.int32,
    )
    owner_index = stored // local_rows
    local_row = stored % local_rows
    slot_labels = jnp.arange(seq_count, dtype=jnp.int32)
    asked_rows = jnp.sum(
        jnp.where(owner_index[:, None] == slot_labels[None, :], local_row[:, None], 0),
        axis=0,
        dtype=jnp.int32,
    )
    wanted = lax.all_to_all(
        asked_rows.reshape(seq_count, 1), "seq", split_axis=0, concat_axis=0, tiled=True
    ).reshape(-1)

    weight = jnp.concatenate([key_weight, value_weight], axis=1)
    along_z = [[y * Z + z for z in range(Z)] for y in range(y_count)]
    along_y = [[y * Z + z for y in range(y_count)] for z in range(Z)]
    weight = lax.all_gather(weight, "seq", axis=0, tiled=True, axis_index_groups=along_z)
    first_rows = shifted(
        jnp.concatenate([queries[:margin], context_grad[:margin]], axis=1), "seq", -1
    )

    parts = database.reshape(local_rows, head_devices, part_tokens, enc_width)
    mine = lax.dynamic_index_in_dim(parts, my_head, axis=1, keepdims=False)
    wanted, weight, first_rows = lax.optimization_barrier((wanted, weight, first_rows))
    weight = lax.all_gather(weight, "seq", axis=0, tiled=True, axis_index_groups=along_y)
    pieces = []
    start = 0
    for width in PIECES:
        outgoing = mine[:, :, start : start + width][wanted]
        incoming = lax.all_to_all(outgoing, "seq", split_axis=0, concat_axis=0, tiled=True)
        asked = incoming[owner_index]
        rows = lax.all_gather(asked, "head", axis=0, tiled=False)
        pieces.append(rows.reshape(head_devices, -1, 2 * part_tokens, width))
        start += width

    width = queries.shape[1]
    shifted_queries = jnp.concatenate([queries[margin:], first_rows[:, :width]], axis=0)
    shifted_grads = jnp.concatenate([context_grad[margin:], first_rows[:, width:]], axis=0)
    return attention(shifted_queries, shifted_grads, pieces, weight)


def solution(mesh):
    return jax.shard_map(
        body,
        mesh=mesh,
        in_specs=(
            P("seq", "head"),
            P("seq", "head"),
            P("seq", None, None),
            P("seq", None),
            P(),
            P("seq", "head"),
            P("seq", "head"),
        ),
        out_specs=(P("seq", "head"), P("seq", "head")),
        check_vma=False,
    )
```

```python
import jax
import jax.numpy as jnp
from jax import lax
from jax.experimental import pallas as pl
from jax.experimental.pallas import tpu as pltpu
from jax.sharding import PartitionSpec as P

DH = 128
BLOCK = 64


def shifted(value, axis, steps):
    count = lax.axis_size(axis)
    first, last = (max(0, -steps), min(count, count - steps))
    return lax.ppermute(value, axis, [(source, source + steps) for source in range(first, last)])


def attend(query, grad, key, value):
    scale = DH ** (-0.5)
    last = (((1,), (1,)), ((), ()))
    scores = lax.dot_general(query, key, last, preferred_element_type=jnp.float32) * scale
    prob_grad = lax.dot_general(grad, value, last, preferred_element_type=jnp.float32)
    weights = jnp.exp(scores - jnp.max(scores, axis=-1, keepdims=True))
    probabilities = weights / jnp.sum(weights, axis=-1, keepdims=True)
    context = jnp.dot(
        probabilities.astype(jnp.bfloat16), value, preferred_element_type=jnp.float32
    )
    delta = jnp.sum(probabilities * prob_grad, axis=-1, keepdims=True)
    dscore = (probabilities * (prob_grad - delta) * scale).astype(jnp.bfloat16)
    qgrad = jnp.dot(dscore, key, preferred_element_type=jnp.float32)
    return context.astype(jnp.bfloat16), qgrad.astype(jnp.bfloat16)


def attend_kernel(tokens_ref, rows_ref, weight_ref, out_ref, kv_ref):
    width = tokens_ref.shape[2] // 2
    rows = rows_ref[...].reshape(-1, rows_ref.shape[-1])
    kv = jnp.dot(rows, weight_ref[0], preferred_element_type=jnp.float32)
    kv_ref[...] = kv.astype(jnp.bfloat16).reshape(kv_ref.shape)
    for at in range(rows_ref.shape[1]):
        place = slice(at * BLOCK, (at + 1) * BLOCK)
        for head in range(width // DH):
            own = slice(head * DH, (head + 1) * DH)
            other = slice(width + head * DH, width + (head + 1) * DH)
            key = kv_ref[:, at, :, own].reshape(-1, DH)
            value = kv_ref[:, at, :, other].reshape(-1, DH)
            context, qgrad = attend(
                tokens_ref[0, place, own], tokens_ref[0, place, other], key, value
            )
            out_ref[0, place, own] = context
            out_ref[0, place, other] = qgrad


def attention(tokens, rows, weights):
    parts, count, double = tokens.shape
    row_parts, blocks, part_tokens, enc_width = rows.shape
    keys = row_parts * part_tokens
    place = pl.BlockSpec((1, count, double), lambda i: (i, 0, 0))
    return pl.pallas_call(
        attend_kernel,
        grid=(parts,),
        out_shape=jax.ShapeDtypeStruct(tokens.shape, jnp.bfloat16),
        in_specs=[
            place,
            pl.BlockSpec(rows.shape, lambda i: (0, 0, 0, 0)),
            pl.BlockSpec((1, enc_width, double), lambda i: (i, 0, 0)),
        ],
        out_specs=place,
        scratch_shapes=[pltpu.VMEM((row_parts, blocks, part_tokens, double), jnp.bfloat16)],
        compiler_params=pltpu.CompilerParams(vmem_limit_bytes=56 * 1024 * 1024),
        cost_estimate=pl.CostEstimate(
            flops=2 * parts * blocks * keys * double * (enc_width + 2 * BLOCK),
            bytes_accessed=2 * (2 * tokens.size + rows.size + weights.size),
            transcendentals=parts * blocks * keys * BLOCK * double // (2 * DH),
        ),
        name="blocks",
    )(tokens, rows, weights)


def body(queries, context_grad, database, neighbour_ids, owner_map, key_weight, value_weight):
    margin = BLOCK - 1
    width = queries.shape[1]
    seq_count = lax.axis_size("seq")
    head_devices = lax.axis_size("head")
    local_rows, neigh_tokens, enc_width = database.shape
    part_tokens = neigh_tokens // head_devices
    my_head = lax.axis_index("head")

    weight = jnp.concatenate([key_weight, value_weight], axis=1)
    weight = lax.all_gather(weight, "seq", axis=0, tiled=True)
    weights = lax.all_gather(weight, "head", axis=0, tiled=False)

    request_ids = neighbour_ids.reshape(-1)
    row_labels = jnp.arange(owner_map.shape[0], dtype=jnp.int32)
    stored = jnp.sum(
        jnp.where(request_ids[:, None] == row_labels[None, :], owner_map[None, :], 0),
        axis=1,
        dtype=jnp.int32,
    )
    owner_index = stored // local_rows
    local_row = stored % local_rows
    slot_labels = jnp.arange(seq_count, dtype=jnp.int32)
    asked_rows = jnp.sum(
        jnp.where(owner_index[:, None] == slot_labels[None, :], local_row[:, None], 0),
        axis=0,
        dtype=jnp.int32,
    )
    wanted = lax.all_to_all(
        asked_rows.reshape(seq_count, 1), "seq", split_axis=0, concat_axis=0, tiled=True
    ).reshape(-1)

    tokens = jnp.concatenate([queries, context_grad], axis=1)
    tokens = jnp.concatenate([tokens[margin:], shifted(tokens[:margin], "seq", -1)], axis=0)
    tokens = lax.all_to_all(
        tokens.reshape(head_devices, -1, 2 * width), "head", split_axis=0, concat_axis=0, tiled=True
    )

    parts = database.reshape(local_rows, head_devices, part_tokens, enc_width)
    mine = lax.dynamic_index_in_dim(parts, my_head, axis=1, keepdims=False)
    wanted, tokens = lax.optimization_barrier((wanted, tokens))
    outgoing = mine[wanted]
    incoming = lax.all_to_all(outgoing, "seq", split_axis=0, concat_axis=0, tiled=True)
    asked = incoming[owner_index]
    rows = lax.all_to_all(
        asked.reshape(head_devices, -1, part_tokens, enc_width),
        "head",
        split_axis=0,
        concat_axis=0,
        tiled=True,
    )
    blocks = rows.shape[1] // 2
    rows = rows.reshape(head_devices, blocks, 2 * part_tokens, enc_width)

    out = attention(tokens, rows, weights)
    out = lax.all_to_all(out, "head", split_axis=0, concat_axis=0, tiled=True)
    out = out.reshape(-1, 2 * width)
    first = shifted(out[-margin:], "seq", 1)
    context = jnp.concatenate([first[:, :width], out[:-margin, :width]], axis=0)
    query_grad = jnp.concatenate([first[:, width:], out[:-margin, width:]], axis=0)
    return context, query_grad


def solution(mesh):
    return jax.shard_map(
        body,
        mesh=mesh,
        in_specs=(
            P("seq", "head"),
            P("seq", "head"),
            P("seq", None, None),
            P("seq", None),
            P(),
            P("seq", "head"),
            P("seq", "head"),
        ),
        out_specs=(P("seq", "head"), P("seq", "head")),
        check_vma=False,
    )
```

```python
import functools

import jax
import jax.numpy as jnp
from jax import lax
from jax.experimental import pallas as pl
from jax.experimental.pallas import tpu as pltpu
from jax.sharding import PartitionSpec as P

DH = 128
BLOCK = 64
FEATURES = 1024
Z = 16
GROUP = 4


def shifted(value, axis, steps):
    count = lax.axis_size(axis)
    first, last = (max(0, -steps), min(count, count - steps))
    return lax.ppermute(value, axis, [(source, source + steps) for source in range(first, last)])


def scores_of(left, right):
    last = (((1,), (1,)), ((), ()))
    return lax.dot_general(left, right, last, preferred_element_type=jnp.float32)


def grouped(refs):
    groups = []
    for ref in refs:
        if groups and groups[-1][0].shape[-1] < FEATURES and len(groups[-1]) == 1:
            groups[-1].append(ref)
        else:
            groups.append([ref])
    return groups


def project(piece_refs, weight_ref, kv_ref):
    rows = []
    for group in grouped(piece_refs):
        parts = [ref[...].reshape(-1, ref.shape[-1]) for ref in group]
        rows.append(parts[0] if len(parts) == 1 else jnp.concatenate(parts, axis=1))
    kv = jnp.dot(
        jnp.concatenate(rows, axis=0), weight_ref[...], preferred_element_type=jnp.float32
    )
    kv_ref[...] = kv.astype(jnp.bfloat16).reshape(kv_ref.shape)


def attend(queries, grads, kv_ref):
    scale = DH ** (-0.5)
    width = queries[0].shape[1]
    pairs = [(at, head) for at in range(len(queries)) for head in range(width // DH)]
    keys, values, scores, prob_grad = [], [], [], []
    for at, head in pairs:
        own = slice(head * DH, (head + 1) * DH)
        other = slice(width + head * DH, width + (head + 1) * DH)
        keys.append(kv_ref[:, at, :, own].reshape(-1, DH))
        values.append(kv_ref[:, at, :, other].reshape(-1, DH))
        scores.append(scores_of(queries[at][:, own], keys[-1]))
        prob_grad.append(scores_of(grads[at][:, own], values[-1]))
    scores = jnp.concatenate(scores, axis=0) * scale
    prob_grad = jnp.concatenate(prob_grad, axis=0)
    weights = jnp.exp(scores - jnp.max(scores, axis=-1, keepdims=True))
    probabilities = weights / jnp.sum(weights, axis=-1, keepdims=True)
    delta = jnp.sum(probabilities * prob_grad, axis=-1, keepdims=True)
    probs_low = probabilities.astype(jnp.bfloat16)
    dscore = (probabilities * (prob_grad - delta) * scale).astype(jnp.bfloat16)
    blocks = [([], []) for _ in queries]
    for i, (at, head) in enumerate(pairs):
        rows = slice(i * BLOCK, (i + 1) * BLOCK)
        blocks[at][0].append(jnp.dot(probs_low[rows], values[i], preferred_element_type=jnp.float32))
        blocks[at][1].append(jnp.dot(dscore[rows], keys[i], preferred_element_type=jnp.float32))
    return [tuple(jnp.concatenate(heads, axis=1) for heads in block) for block in blocks]


def block_rows(ref, next_ref, at, count, last_row):
    here = ref[at * BLOCK : (at + 1) * BLOCK, :]
    there = next_ref[...] if at + 1 == count else ref[(at + 1) * BLOCK : (at + 2) * BLOCK, :]
    rows = jnp.where(last_row, here.astype(jnp.float32), there.astype(jnp.float32))
    return rows.astype(jnp.bfloat16)


def main_kernel(pieces_count, place_ref, query_ref, next_query_ref, grad_ref, next_grad_ref, *refs):
    piece_refs, refs = refs[:pieces_count], refs[pieces_count:]
    before_refs, refs = refs[:pieces_count], refs[pieces_count:]
    *held_refs, context_ref, qgrad_ref, weight_ref, kv_ref, before_kv_ref, carry_ref = refs

    @pl.when(pl.program_id(0) == 0)
    def _():
        rows = held_refs[0].shape[1]
        for step, held_ref in enumerate(held_refs):
            y = lax.rem(place_ref[0] + len(held_refs) - step, len(held_refs))
            for m in range(Z):
                at = (m & 3) * 4 + (m >> 2 & 1) * 2 + (m >> 3)
                start = (y * Z + (place_ref[1] ^ m)) * rows
                weight_ref[pl.ds(pl.multiple_of(start, 16), rows), :] = held_ref[at]
        project(before_refs, weight_ref, before_kv_ref)
        ((context, qgrad),) = attend([query_ref[:BLOCK, :]], [grad_ref[:BLOCK, :]], before_kv_ref)
        carry_ref[0] = context
        carry_ref[1] = qgrad

    project(piece_refs, weight_ref, kv_ref)
    count = kv_ref.shape[1]
    row = lax.broadcasted_iota(jnp.int32, (BLOCK, query_ref.shape[1]), 0)
    last_row = row == BLOCK - 1
    queries = [block_rows(query_ref, next_query_ref, at, count, last_row) for at in range(count)]
    grads = [block_rows(grad_ref, next_grad_ref, at, count, last_row) for at in range(count)]
    before = carry_ref[0], carry_ref[1]
    for at, now in enumerate(attend(queries, grads, kv_ref)):
        for out_ref, old, new in zip((context_ref, qgrad_ref), before, now):
            tile = jnp.where(last_row, new, old)
            out_ref[at * BLOCK : (at + 1) * BLOCK, :] = tile.astype(jnp.bfloat16)
        before = now
    carry_ref[0], carry_ref[1] = before


def attention(place, queries, grads, pieces, held):
    tokens, width = queries.shape
    blocks = tokens // BLOCK
    part_tokens = pieces[0].shape[1]
    parts = sum(p.shape[-1] for p in pieces) // FEATURES
    keys = parts * part_tokens
    tile = pl.BlockSpec((GROUP * BLOCK, width), lambda i: (i, 0))
    next_tile = pl.BlockSpec(
        (BLOCK, width), lambda i: (jnp.minimum((i + 1) * GROUP, blocks - 1), 0)
    )

    def whole(value):
        return pl.BlockSpec(value.shape, lambda i: (0,) * value.ndim)

    def kv_scratch(group):
        return pltpu.VMEM((parts, group, part_tokens, 2 * width), jnp.bfloat16)

    out = jax.ShapeDtypeStruct((tokens, width), jnp.bfloat16)
    return pl.pallas_call(
        functools.partial(main_kernel, len(pieces)),
        grid=(blocks // GROUP,),
        out_shape=(out, out),
        in_specs=[pl.BlockSpec(memory_space=pltpu.SMEM), tile, next_tile, tile, next_tile]
        + [pl.BlockSpec((GROUP,) + p.shape[1:], lambda i: (i, 0, 0)) for p in pieces]
        + [pl.BlockSpec((1,) + p.shape[1:], lambda i: (blocks, 0, 0)) for p in pieces]
        + [whole(h) for h in held],
        out_specs=(tile, tile),
        scratch_shapes=[
            pltpu.VMEM((FEATURES, 2 * width), jnp.bfloat16),
            kv_scratch(GROUP),
            kv_scratch(1),
            pltpu.VMEM((2, BLOCK, width), jnp.float32),
        ],
        compiler_params=pltpu.CompilerParams(vmem_limit_bytes=32 * 1024 * 1024),
        cost_estimate=pl.CostEstimate(
            flops=2 * (blocks + 1) * keys * 2 * width * (FEATURES + 2 * BLOCK),
            bytes_accessed=2 * (blocks * keys * FEATURES + 4 * tokens * width),
            transcendentals=blocks * keys * BLOCK * width // DH,
        ),
        name="blocks",
    )(place, queries, queries, grads, grads, *pieces, *pieces, *held)


def body(queries, context_grad, database, neighbour_ids, owner_map, key_weight, value_weight):
    seq_count = lax.axis_size("seq")
    head_devices = lax.axis_size("head")
    y_count = seq_count // Z
    local_rows, neigh_tokens, enc_width = database.shape
    part_tokens = neigh_tokens // head_devices
    my_head = lax.axis_index("head")

    request_ids = neighbour_ids.reshape(-1)
    row_labels = jnp.arange(owner_map.shape[0], dtype=jnp.int32)
    stored = jnp.sum(
        jnp.where(request_ids[:, None] == row_labels[None, :], owner_map[None, :], 0),
        axis=1,
        dtype=jnp.int32,
    )
    owner_index = stored // local_rows
    local_row = stored % local_rows
    slot_labels = jnp.arange(seq_count, dtype=jnp.int32)
    asked_rows = jnp.sum(
        jnp.where(owner_index[:, None] == slot_labels[None, :], local_row[:, None], 0),
        axis=0,
        dtype=jnp.int32,
    )
    wanted = lax.all_to_all(
        asked_rows.reshape(seq_count, 1), "seq", split_axis=0, concat_axis=0, tiled=True
    ).reshape(-1)

    def from_z(value, step):
        return lax.ppermute(value, "seq", [(i, i ^ step) for i in range(seq_count)])

    weight = jnp.concatenate([key_weight, value_weight], axis=1)[None]
    for step in (8, 4):
        weight = jnp.concatenate([weight, from_z(weight, step)], axis=0)

    parts = database.reshape(local_rows, head_devices, part_tokens, enc_width)
    mine = lax.dynamic_index_in_dim(parts, my_head, axis=1, keepdims=False)
    wanted, weight = lax.optimization_barrier((wanted, weight))
    outgoing = mine[wanted]
    outgoing, weight = lax.optimization_barrier((outgoing, weight))
    incoming = lax.all_to_all(outgoing, "seq", split_axis=0, concat_axis=0, tiled=True)
    weight = jnp.concatenate([weight] + [from_z(weight, step) for step in (1, 2, 3)], axis=0)
    asked = incoming[owner_index]
    weight, asked = lax.optimization_barrier((weight, asked))
    asked = jnp.concatenate([asked, shifted(asked[-2:], "seq", 1)], axis=0)

    def along_x(value, steps):
        return lax.ppermute(
            value, "head", [(i, (i + 2 * steps) % head_devices) for i in range(head_devices)]
        )

    def other_core(value):
        return lax.ppermute(value, "head", [(i, i ^ 1) for i in range(head_devices)])

    half = enc_width // 2
    before, after = along_x(asked, 1), along_x(asked, -1)
    across = along_x(before[:, :, :half], 1), along_x(after[:, :, half:], -1)
    pieces = [asked, before, after, *across]
    pieces += [other_core(piece) for piece in pieces]
    pieces = [piece.reshape(-1, 2 * part_tokens, piece.shape[-1]) for piece in pieces]

    held = [weight]
    for step in range(1, y_count):
        pairs = [(i, (i + step * Z) % seq_count) for i in range(seq_count)]
        held.append(lax.ppermute(weight, "seq", pairs))
    my_seq = lax.axis_index("seq")
    place = jnp.stack([my_seq // Z, my_seq % Z]).astype(jnp.int32)
    return attention(place, queries, context_grad, pieces, held)


def solution(mesh):
    return jax.shard_map(
        body,
        mesh=mesh,
        in_specs=(
            P("seq", "head"),
            P("seq", "head"),
            P("seq", None, None),
            P("seq", None),
            P(),
            P("seq", "head"),
            P("seq", "head"),
        ),
        out_specs=(P("seq", "head"), P("seq", "head")),
        check_vma=False,
    )
```

```python
import jax
import jax.numpy as jnp
from jax import lax
from jax.experimental import pallas as pl
from jax.experimental.pallas import tpu as pltpu
from jax.sharding import PartitionSpec as P

DH = 128
BLOCK = 64
FEATURES = 1024
FIRST, SECOND = 640, 384
Z = 16
GROUP = 4


def shifted(value, axis, steps):
    count = lax.axis_size(axis)
    first, last = (max(0, -steps), min(count, count - steps))
    return lax.ppermute(value, axis, [(source, source + steps) for source in range(first, last)])


def scores_of(left, right):
    last = (((1,), (1,)), ((), ()))
    return lax.dot_general(left, right, last, preferred_element_type=jnp.float32)


def project(rows, weight_ref, kv_ref):
    rows = jnp.concatenate([part.reshape(-1, part.shape[-1]) for part in rows], axis=1)
    kv = jnp.dot(rows, weight_ref[...], preferred_element_type=jnp.float32)
    kv_ref[...] = kv.astype(jnp.bfloat16).reshape(kv_ref.shape)


def attend(queries, grads, kv_ref):
    scale = DH ** (-0.5)
    width = queries[0].shape[1]
    pairs = [(at, head) for at in range(len(queries)) for head in range(width // DH)]
    keys, values, scores, prob_grad = [], [], [], []
    for at, head in pairs:
        own = slice(head * DH, (head + 1) * DH)
        other = slice(width + head * DH, width + (head + 1) * DH)
        keys.append(kv_ref[:, at, :, own].reshape(-1, DH))
        values.append(kv_ref[:, at, :, other].reshape(-1, DH))
        scores.append(scores_of(queries[at][:, own], keys[-1]))
        prob_grad.append(scores_of(grads[at][:, own], values[-1]))
    scores = jnp.concatenate(scores, axis=0) * scale
    prob_grad = jnp.concatenate(prob_grad, axis=0)
    weights = jnp.exp(scores - jnp.max(scores, axis=-1, keepdims=True))
    probabilities = weights / jnp.sum(weights, axis=-1, keepdims=True)
    delta = jnp.sum(probabilities * prob_grad, axis=-1, keepdims=True)
    probs_low = probabilities.astype(jnp.bfloat16)
    dscore = (probabilities * (prob_grad - delta) * scale).astype(jnp.bfloat16)
    blocks = [([], []) for _ in queries]
    for i, (at, head) in enumerate(pairs):
        rows = slice(i * BLOCK, (i + 1) * BLOCK)
        blocks[at][0].append(jnp.dot(probs_low[rows], values[i], preferred_element_type=jnp.float32))
        blocks[at][1].append(jnp.dot(dscore[rows], keys[i], preferred_element_type=jnp.float32))
    return [tuple(jnp.concatenate(heads, axis=1) for heads in block) for block in blocks]


def block_rows(ref, next_ref, at, count, last_row):
    here = ref[at * BLOCK : (at + 1) * BLOCK, :]
    there = next_ref[...] if at + 1 == count else ref[(at + 1) * BLOCK : (at + 2) * BLOCK, :]
    rows = jnp.where(last_row, here.astype(jnp.float32), there.astype(jnp.float32))
    return rows.astype(jnp.bfloat16)


def main_kernel(
    place_ref,
    query_ref,
    next_query_ref,
    grad_ref,
    next_grad_ref,
    first_ref,
    second_ref,
    before_second_ref,
    before_low_ref,
    before_high_ref,
    *refs,
):
    *held_refs, context_ref, qgrad_ref, weight_ref, kv_ref, before_kv_ref, carry_ref = refs

    @pl.when(pl.program_id(0) == 0)
    def _():
        rows = held_refs[0].shape[1]
        for step, held_ref in enumerate(held_refs):
            y = lax.rem(place_ref[0] + len(held_refs) - step, len(held_refs))
            for m in range(Z):
                at = (m & 3) * 4 + (m >> 2 & 1) * 2 + (m >> 3)
                start = (y * Z + (place_ref[1] ^ m)) * rows
                weight_ref[pl.ds(pl.multiple_of(start, 16), rows), :] = held_ref[at]
        high = before_high_ref[:, :, :, : FIRST - SECOND]
        rows = [before_low_ref[...], high, before_second_ref[...]]
        project(rows, weight_ref, before_kv_ref)
        ((context, qgrad),) = attend([query_ref[:BLOCK, :]], [grad_ref[:BLOCK, :]], before_kv_ref)
        carry_ref[0] = context
        carry_ref[1] = qgrad

    project([first_ref[...], second_ref[...]], weight_ref, kv_ref)
    count = kv_ref.shape[1]
    row = lax.broadcasted_iota(jnp.int32, (BLOCK, query_ref.shape[1]), 0)
    last_row = row == BLOCK - 1
    queries = [block_rows(query_ref, next_query_ref, at, count, last_row) for at in range(count)]
    grads = [block_rows(grad_ref, next_grad_ref, at, count, last_row) for at in range(count)]
    before = carry_ref[0], carry_ref[1]
    for at, now in enumerate(attend(queries, grads, kv_ref)):
        for out_ref, old, new in zip((context_ref, qgrad_ref), before, now):
            tile = jnp.where(last_row, new, old)
            out_ref[at * BLOCK : (at + 1) * BLOCK, :] = tile.astype(jnp.bfloat16)
        before = now
    carry_ref[0], carry_ref[1] = before


def attention(place, queries, grads, first, second, held):
    tokens, width = queries.shape
    blocks = tokens // BLOCK
    parts, _, part_tokens, _ = first.shape
    keys = parts * part_tokens
    tile = pl.BlockSpec((GROUP * BLOCK, width), lambda i: (i, 0))
    next_tile = pl.BlockSpec(
        (BLOCK, width), lambda i: (jnp.minimum((i + 1) * GROUP, blocks - 1), 0)
    )

    def group_of(value):
        return pl.BlockSpec((parts, GROUP, part_tokens, value.shape[-1]), lambda i: (0, i, 0, 0))

    def one_of(value, at):
        return pl.BlockSpec((parts, 1, part_tokens, value.shape[-1]), lambda i: (0, at, 0, 0))

    def whole(value):
        return pl.BlockSpec(value.shape, lambda i: (0,) * value.ndim)

    def kv_scratch(group):
        return pltpu.VMEM((parts, group, part_tokens, 2 * width), jnp.bfloat16)

    out = jax.ShapeDtypeStruct((tokens, width), jnp.bfloat16)
    return pl.pallas_call(
        main_kernel,
        grid=(blocks // GROUP,),
        out_shape=(out, out),
        in_specs=[pl.BlockSpec(memory_space=pltpu.SMEM), tile, next_tile, tile, next_tile]
        + [group_of(first), group_of(second)]
        + [one_of(second, blocks + k) for k in range(3)]
        + [whole(h) for h in held],
        out_specs=(tile, tile),
        scratch_shapes=[
            pltpu.VMEM((FEATURES, 2 * width), jnp.bfloat16),
            kv_scratch(GROUP),
            kv_scratch(1),
            pltpu.VMEM((2, BLOCK, width), jnp.float32),
        ],
        compiler_params=pltpu.CompilerParams(vmem_limit_bytes=56 * 1024 * 1024),
        cost_estimate=pl.CostEstimate(
            flops=2 * (blocks + 1) * keys * 2 * width * (FEATURES + 2 * BLOCK),
            bytes_accessed=2 * (blocks * keys * FEATURES + 4 * tokens * width),
            transcendentals=blocks * keys * BLOCK * width // DH,
        ),
        name="blocks",
    )(
        place, queries, queries, grads, grads, first, second, second, second, second, *held
    )


def body(queries, context_grad, database, neighbour_ids, owner_map, key_weight, value_weight):
    seq_count = lax.axis_size("seq")
    head_devices = lax.axis_size("head")
    y_count = seq_count // Z
    local_rows, neigh_tokens, enc_width = database.shape
    part_tokens = neigh_tokens // head_devices
    my_head = lax.axis_index("head")

    request_ids = neighbour_ids.reshape(-1)
    row_labels = jnp.arange(owner_map.shape[0], dtype=jnp.int32)
    stored = jnp.sum(
        jnp.where(request_ids[:, None] == row_labels[None, :], owner_map[None, :], 0),
        axis=1,
        dtype=jnp.int32,
    )
    owner_index = stored // local_rows
    local_row = stored % local_rows
    slot_labels = jnp.arange(seq_count, dtype=jnp.int32)
    asked_rows = jnp.sum(
        jnp.where(owner_index[:, None] == slot_labels[None, :], local_row[:, None], 0),
        axis=0,
        dtype=jnp.int32,
    )
    wanted = lax.all_to_all(
        asked_rows.reshape(seq_count, 1), "seq", split_axis=0, concat_axis=0, tiled=True
    ).reshape(-1)

    def from_z(value, step):
        return lax.ppermute(value, "seq", [(i, i ^ step) for i in range(seq_count)])

    weight = jnp.concatenate([key_weight, value_weight], axis=1)[None]
    for step in (8, 4):
        weight = jnp.concatenate([weight, from_z(weight, step)], axis=0)

    parts = database.reshape(local_rows, head_devices, part_tokens, enc_width)
    mine = lax.dynamic_index_in_dim(parts, my_head, axis=1, keepdims=False)
    wanted, weight = lax.optimization_barrier((wanted, weight))

    def exchanged(start, stop, wanted):
        outgoing = mine[:, :, start:stop][wanted]
        incoming = lax.all_to_all(outgoing, "seq", split_axis=0, concat_axis=0, tiled=True)
        return incoming[owner_index]

    def all_parts(rows):
        rows = lax.all_gather(rows, "head", axis=0, tiled=False)
        return rows.reshape(head_devices, -1, 2 * part_tokens, rows.shape[-1])

    asked_first = exchanged(0, FIRST, wanted)
    weight = jnp.concatenate([weight] + [from_z(weight, step) for step in (1, 2, 3)], axis=0)
    first = all_parts(asked_first)
    asked_first, wanted = lax.optimization_barrier((asked_first, wanted))
    asked_second = exchanged(FIRST, FEATURES, wanted)
    weight, asked_second, first = lax.optimization_barrier((weight, asked_second, first))
    last = jnp.concatenate([asked_first[-2:], asked_second[-2:]], axis=-1)
    last = shifted(last, "seq", 1)
    high = jnp.pad(last[:, :, SECOND:FIRST], ((0, 0), (0, 0), (0, 2 * SECOND - FIRST)))
    second = all_parts(
        jnp.concatenate([asked_second, last[:, :, FIRST:], last[:, :, :SECOND], high], axis=0)
    )

    held = [weight]
    for step in range(1, y_count):
        pairs = [(i, (i + step * Z) % seq_count) for i in range(seq_count)]
        held.append(lax.ppermute(weight, "seq", pairs))
    my_seq = lax.axis_index("seq")
    place = jnp.stack([my_seq // Z, my_seq % Z]).astype(jnp.int32)
    return attention(place, queries, context_grad, first, second, held)


def solution(mesh):
    return jax.shard_map(
        body,
        mesh=mesh,
        in_specs=(
            P("seq", "head"),
            P("seq", "head"),
            P("seq", None, None),
            P("seq", None),
            P(),
            P("seq", "head"),
            P("seq", "head"),
        ),
        out_specs=(P("seq", "head"), P("seq", "head")),
        check_vma=False,
    )
```

```python
import functools

import jax
import jax.numpy as jnp
from jax import lax
from jax.experimental import pallas as pl
from jax.experimental.pallas import tpu as pltpu
from jax.sharding import PartitionSpec as P

DH = 128
BLOCK = 64
FEATURES = 1024
Z = 16
GROUP = 4


def shifted(value, axis, steps):
    count = lax.axis_size(axis)
    first, last = (max(0, -steps), min(count, count - steps))
    return lax.ppermute(value, axis, [(source, source + steps) for source in range(first, last)])


def scores_of(left, right):
    last = (((1,), (1,)), ((), ()))
    return lax.dot_general(left, right, last, preferred_element_type=jnp.float32)


def grouped(refs):
    groups = []
    for ref in refs:
        if groups and groups[-1][0].shape[-1] < FEATURES and len(groups[-1]) == 1:
            groups[-1].append(ref)
        else:
            groups.append([ref])
    return groups


def project(piece_refs, weight_ref, kv_ref):
    rows = []
    for group in grouped(piece_refs):
        parts = [ref[...].reshape(-1, ref.shape[-1]) for ref in group]
        rows.append(parts[0] if len(parts) == 1 else jnp.concatenate(parts, axis=1))
    kv = jnp.dot(
        jnp.concatenate(rows, axis=0), weight_ref[...], preferred_element_type=jnp.float32
    )
    kv_ref[...] = kv.astype(jnp.bfloat16).reshape(kv_ref.shape)


def attend(queries, grads, kv_ref):
    scale = DH ** (-0.5)
    width = queries[0].shape[1]
    pairs = [(at, head) for at in range(len(queries)) for head in range(width // DH)]
    keys, values, scores, prob_grad = [], [], [], []
    for at, head in pairs:
        own = slice(head * DH, (head + 1) * DH)
        other = slice(width + head * DH, width + (head + 1) * DH)
        keys.append(kv_ref[:, at, :, own].reshape(-1, DH))
        values.append(kv_ref[:, at, :, other].reshape(-1, DH))
        scores.append(scores_of(queries[at][:, own], keys[-1]))
        prob_grad.append(scores_of(grads[at][:, own], values[-1]))
    scores = jnp.concatenate(scores, axis=0) * scale
    prob_grad = jnp.concatenate(prob_grad, axis=0)
    weights = jnp.exp(scores - jnp.max(scores, axis=-1, keepdims=True))
    probabilities = weights / jnp.sum(weights, axis=-1, keepdims=True)
    delta = jnp.sum(probabilities * prob_grad, axis=-1, keepdims=True)
    probs_low = probabilities.astype(jnp.bfloat16)
    dscore = (probabilities * (prob_grad - delta) * scale).astype(jnp.bfloat16)
    blocks = [([], []) for _ in queries]
    for i, (at, head) in enumerate(pairs):
        rows = slice(i * BLOCK, (i + 1) * BLOCK)
        blocks[at][0].append(jnp.dot(probs_low[rows], values[i], preferred_element_type=jnp.float32))
        blocks[at][1].append(jnp.dot(dscore[rows], keys[i], preferred_element_type=jnp.float32))
    return [tuple(jnp.concatenate(heads, axis=1) for heads in block) for block in blocks]


def block_rows(ref, next_ref, at, count, last_row):
    here = ref[at * BLOCK : (at + 1) * BLOCK, :]
    there = next_ref[...] if at + 1 == count else ref[(at + 1) * BLOCK : (at + 2) * BLOCK, :]
    rows = jnp.where(last_row, here.astype(jnp.float32), there.astype(jnp.float32))
    return rows.astype(jnp.bfloat16)


def main_kernel(pieces_count, place_ref, query_ref, next_query_ref, grad_ref, next_grad_ref, *refs):
    piece_refs, refs = refs[:pieces_count], refs[pieces_count:]
    before_refs, refs = refs[:pieces_count], refs[pieces_count:]
    *held_refs, context_ref, qgrad_ref, weight_ref, kv_ref, before_kv_ref, carry_ref = refs

    @pl.when(pl.program_id(0) == 0)
    def _():
        rows = held_refs[0].shape[1]
        for step, held_ref in enumerate(held_refs):
            y = lax.rem(place_ref[0] + len(held_refs) - step, len(held_refs))
            for m in range(Z):
                at = (m & 3) * 4 + (m >> 2 & 1) * 2 + (m >> 3)
                start = (y * Z + (place_ref[1] ^ m)) * rows
                weight_ref[pl.ds(pl.multiple_of(start, 16), rows), :] = held_ref[at]
        project(before_refs, weight_ref, before_kv_ref)
        ((context, qgrad),) = attend([query_ref[:BLOCK, :]], [grad_ref[:BLOCK, :]], before_kv_ref)
        carry_ref[0] = context
        carry_ref[1] = qgrad

    project(piece_refs, weight_ref, kv_ref)
    count = kv_ref.shape[1]
    row = lax.broadcasted_iota(jnp.int32, (BLOCK, query_ref.shape[1]), 0)
    last_row = row == BLOCK - 1
    queries = [block_rows(query_ref, next_query_ref, at, count, last_row) for at in range(count)]
    grads = [block_rows(grad_ref, next_grad_ref, at, count, last_row) for at in range(count)]
    before = carry_ref[0], carry_ref[1]
    for at, now in enumerate(attend(queries, grads, kv_ref)):
        for out_ref, old, new in zip((context_ref, qgrad_ref), before, now):
            tile = jnp.where(last_row, new, old)
            out_ref[at * BLOCK : (at + 1) * BLOCK, :] = tile.astype(jnp.bfloat16)
        before = now
    carry_ref[0], carry_ref[1] = before


def attention(place, queries, grads, pieces, held):
    tokens, width = queries.shape
    blocks = tokens // BLOCK
    arrays = [array for array, _, _ in pieces]
    part_tokens = arrays[0].shape[1]
    parts = sum(a.shape[-1] for a in arrays) // FEATURES
    keys = parts * part_tokens
    tile = pl.BlockSpec((GROUP * BLOCK, width), lambda i: (i, 0))
    next_tile = pl.BlockSpec(
        (BLOCK, width), lambda i: (jnp.minimum((i + 1) * GROUP, blocks - 1), 0)
    )

    def whole(value):
        return pl.BlockSpec(value.shape, lambda i: (0,) * value.ndim)

    def group_of(array, start, _):
        return pl.BlockSpec((GROUP,) + array.shape[1:], lambda i: (start // GROUP + i, 0, 0))

    def one_of(array, _, at):
        return pl.BlockSpec((1,) + array.shape[1:], lambda i: (at, 0, 0))

    def kv_scratch(group):
        return pltpu.VMEM((parts, group, part_tokens, 2 * width), jnp.bfloat16)

    out = jax.ShapeDtypeStruct((tokens, width), jnp.bfloat16)
    return pl.pallas_call(
        functools.partial(main_kernel, len(pieces)),
        grid=(blocks // GROUP,),
        out_shape=(out, out),
        in_specs=[pl.BlockSpec(memory_space=pltpu.SMEM), tile, next_tile, tile, next_tile]
        + [group_of(*piece) for piece in pieces]
        + [one_of(*piece) for piece in pieces]
        + [whole(h) for h in held],
        out_specs=(tile, tile),
        scratch_shapes=[
            pltpu.VMEM((FEATURES, 2 * width), jnp.bfloat16),
            kv_scratch(GROUP),
            kv_scratch(1),
            pltpu.VMEM((2, BLOCK, width), jnp.float32),
        ],
        compiler_params=pltpu.CompilerParams(vmem_limit_bytes=56 * 1024 * 1024),
        cost_estimate=pl.CostEstimate(
            flops=2 * (blocks + 1) * keys * 2 * width * (FEATURES + 2 * BLOCK),
            bytes_accessed=2 * (blocks * keys * FEATURES + 4 * tokens * width),
            transcendentals=blocks * keys * BLOCK * width // DH,
        ),
        name="blocks",
    )(place, queries, queries, grads, grads, *arrays, *arrays, *held)


def body(queries, context_grad, database, neighbour_ids, owner_map, key_weight, value_weight):
    seq_count = lax.axis_size("seq")
    head_devices = lax.axis_size("head")
    y_count = seq_count // Z
    local_rows, neigh_tokens, enc_width = database.shape
    part_tokens = neigh_tokens // head_devices
    my_head = lax.axis_index("head")

    request_ids = neighbour_ids.reshape(-1)
    row_labels = jnp.arange(owner_map.shape[0], dtype=jnp.int32)
    stored = jnp.sum(
        jnp.where(request_ids[:, None] == row_labels[None, :], owner_map[None, :], 0),
        axis=1,
        dtype=jnp.int32,
    )
    owner_index = stored // local_rows
    local_row = stored % local_rows
    slot_labels = jnp.arange(seq_count, dtype=jnp.int32)
    asked_rows = jnp.sum(
        jnp.where(owner_index[:, None] == slot_labels[None, :], local_row[:, None], 0),
        axis=0,
        dtype=jnp.int32,
    )
    asked_rows, key_weight = lax.optimization_barrier((asked_rows, key_weight))
    wanted = lax.all_to_all(
        asked_rows.reshape(seq_count, 1), "seq", split_axis=0, concat_axis=0, tiled=True
    ).reshape(-1)

    def from_z(value, step):
        return lax.ppermute(value, "seq", [(i, i ^ step) for i in range(seq_count)])

    weight = jnp.concatenate([key_weight, value_weight], axis=1)[None]
    for step in (8, 4):
        weight = jnp.concatenate([weight, from_z(weight, step)], axis=0)

    parts = database.reshape(local_rows, head_devices, part_tokens, enc_width)
    mine = lax.dynamic_index_in_dim(parts, my_head, axis=1, keepdims=False)
    wanted, weight = lax.optimization_barrier((wanted, weight))
    outgoing = mine[wanted]
    outgoing, weight = lax.optimization_barrier((outgoing, weight))
    incoming = lax.all_to_all(outgoing, "seq", split_axis=0, concat_axis=0, tiled=True)
    weight = jnp.concatenate([weight] + [from_z(weight, step) for step in (1, 2, 3)], axis=0)
    asked = incoming[owner_index]
    weight, asked = lax.optimization_barrier((weight, asked))
    asked = jnp.concatenate([asked, shifted(asked[-2:], "seq", 1)], axis=0)

    def along_x(value, steps):
        return lax.ppermute(
            value, "head", [(i, (i + 2 * steps) % head_devices) for i in range(head_devices)]
        )

    def other_core(value):
        return lax.ppermute(value, "head", [(i, i ^ 1) for i in range(head_devices)])

    half = enc_width // 2
    def together(came, own):
        return jnp.concatenate([came[:-2], own[:-2], came[-2:], own[-2:]], axis=0)

    low, high = asked[:, :, :half], asked[:, :, half:]
    before_low, after_high = along_x(low, 1), along_x(high, -1)
    up, down = along_x(together(before_low, high), 1), along_x(together(after_high, low), -1)
    held = []
    for step in range(1, y_count):
        pairs = [(i, (i + step * Z) % seq_count) for i in range(seq_count)]
        held.append(lax.ppermute(weight, "seq", pairs))
    near = [asked, before_low, after_high]
    swapped = [other_core(a) for a in near]
    up, down, swapped, held = lax.optimization_barrier((up, down, swapped, held))
    held = [weight, *held]
    blocks = queries.shape[0] // BLOCK
    pieces = []
    for arrays in (near + [up, down], swapped + [other_core(up), other_core(down)]):
        arrays = [a.reshape(-1, 2 * part_tokens, a.shape[-1]) for a in arrays]
        asked, before_low, after_high, up, down = arrays
        pieces += [(asked, 0, blocks)]
        pieces += [(before_low, 0, blocks), (up, blocks, 2 * blocks + 1)]
        pieces += [(down, blocks, 2 * blocks + 1), (after_high, 0, blocks)]
        pieces += [(up, 0, 2 * blocks), (down, 0, 2 * blocks)]

    my_seq = lax.axis_index("seq")
    place = jnp.stack([my_seq // Z, my_seq % Z]).astype(jnp.int32)
    return attention(place, queries, context_grad, pieces, held)


def solution(mesh):
    return jax.shard_map(
        body,
        mesh=mesh,
        in_specs=(
            P("seq", "head"),
            P("seq", "head"),
            P("seq", None, None),
            P("seq", None),
            P(),
            P("seq", "head"),
            P("seq", "head"),
        ),
        out_specs=(P("seq", "head"), P("seq", "head")),
        check_vma=False,
    )
```

```python
import functools

import jax
import jax.numpy as jnp
from jax import lax
from jax.experimental import pallas as pl
from jax.experimental.pallas import tpu as pltpu
from jax.sharding import PartitionSpec as P

DH = 128
BLOCK = 64
FEATURES = 1024
Z = 16
GROUP = 4


def shifted(value, axis, steps):
    count = lax.axis_size(axis)
    first, last = (max(0, -steps), min(count, count - steps))
    return lax.ppermute(value, axis, [(source, source + steps) for source in range(first, last)])


def scores_of(left, right):
    last = (((1,), (1,)), ((), ()))
    return lax.dot_general(left, right, last, preferred_element_type=jnp.float32)


def grouped(refs):
    groups = []
    for ref in refs:
        if groups and groups[-1][0].shape[-1] < FEATURES and len(groups[-1]) == 1:
            groups[-1].append(ref)
        else:
            groups.append([ref])
    return groups


def project(piece_refs, weight_ref, kv_ref):
    rows = []
    for group in grouped(piece_refs):
        parts = [ref[...].reshape(-1, ref.shape[-1]) for ref in group]
        rows.append(parts[0] if len(parts) == 1 else jnp.concatenate(parts, axis=1))
    kv = jnp.dot(
        jnp.concatenate(rows, axis=0), weight_ref[...], preferred_element_type=jnp.float32
    )
    kv_ref[...] = kv.astype(jnp.bfloat16).reshape(kv_ref.shape)


def attend(queries, grads, kv_ref):
    scale = DH ** (-0.5)
    width = queries[0].shape[1]
    pairs = [(at, head) for at in range(len(queries)) for head in range(width // DH)]
    keys, values, scores, prob_grad = [], [], [], []
    for at, head in pairs:
        own = slice(head * DH, (head + 1) * DH)
        other = slice(width + head * DH, width + (head + 1) * DH)
        keys.append(kv_ref[:, at, :, own].reshape(-1, DH))
        values.append(kv_ref[:, at, :, other].reshape(-1, DH))
        scores.append(scores_of(queries[at][:, own], keys[-1]))
        prob_grad.append(scores_of(grads[at][:, own], values[-1]))
    scores = jnp.concatenate(scores, axis=0) * scale
    prob_grad = jnp.concatenate(prob_grad, axis=0)
    weights = jnp.exp(scores - jnp.max(scores, axis=-1, keepdims=True))
    probabilities = weights / jnp.sum(weights, axis=-1, keepdims=True)
    delta = jnp.sum(probabilities * prob_grad, axis=-1, keepdims=True)
    probs_low = probabilities.astype(jnp.bfloat16)
    dscore = (probabilities * (prob_grad - delta) * scale).astype(jnp.bfloat16)
    blocks = [([], []) for _ in queries]
    for i, (at, head) in enumerate(pairs):
        rows = slice(i * BLOCK, (i + 1) * BLOCK)
        blocks[at][0].append(jnp.dot(probs_low[rows], values[i], preferred_element_type=jnp.float32))
        blocks[at][1].append(jnp.dot(dscore[rows], keys[i], preferred_element_type=jnp.float32))
    return [tuple(jnp.concatenate(heads, axis=1) for heads in block) for block in blocks]


def block_rows(ref, next_ref, at, count, last_row):
    here = ref[at * BLOCK : (at + 1) * BLOCK, :]
    there = next_ref[...] if at + 1 == count else ref[(at + 1) * BLOCK : (at + 2) * BLOCK, :]
    rows = jnp.where(last_row, here.astype(jnp.float32), there.astype(jnp.float32))
    return rows.astype(jnp.bfloat16)


def main_kernel(pieces_count, place_ref, query_ref, next_query_ref, grad_ref, next_grad_ref, *refs):
    piece_refs, refs = refs[:pieces_count], refs[pieces_count:]
    before_refs, refs = refs[:pieces_count], refs[pieces_count:]
    *held_refs, context_ref, qgrad_ref, weight_ref, kv_ref, before_kv_ref, carry_ref = refs

    @pl.when(pl.program_id(0) == 0)
    def _():
        rows = held_refs[0].shape[1]
        y_count = len(held_refs) // 2
        for k, held_ref in enumerate(held_refs):
            y = lax.rem(place_ref[0] + y_count - k // 2, y_count)
            for at in range(held_ref.shape[0]):
                m = (at & 1) * 8 + (at >> 1 & 1) * 4 + (at >> 2) * 2 + k % 2
                start = (y * Z + (place_ref[1] ^ m)) * rows
                weight_ref[pl.ds(pl.multiple_of(start, 16), rows), :] = held_ref[at]
        project(before_refs, weight_ref, before_kv_ref)
        ((context, qgrad),) = attend([query_ref[:BLOCK, :]], [grad_ref[:BLOCK, :]], before_kv_ref)
        carry_ref[0] = context
        carry_ref[1] = qgrad

    project(piece_refs, weight_ref, kv_ref)
    count = kv_ref.shape[1]
    row = lax.broadcasted_iota(jnp.int32, (BLOCK, query_ref.shape[1]), 0)
    last_row = row == BLOCK - 1
    queries = [block_rows(query_ref, next_query_ref, at, count, last_row) for at in range(count)]
    grads = [block_rows(grad_ref, next_grad_ref, at, count, last_row) for at in range(count)]
    before = carry_ref[0], carry_ref[1]
    for at, now in enumerate(attend(queries, grads, kv_ref)):
        for out_ref, old, new in zip((context_ref, qgrad_ref), before, now):
            tile = jnp.where(last_row, new, old)
            out_ref[at * BLOCK : (at + 1) * BLOCK, :] = tile.astype(jnp.bfloat16)
        before = now
    carry_ref[0], carry_ref[1] = before


def attention(place, queries, grads, pieces, held):
    tokens, width = queries.shape
    blocks = tokens // BLOCK
    arrays = [array for array, _, _ in pieces]
    part_tokens = arrays[0].shape[1]
    parts = sum(a.shape[-1] for a in arrays) // FEATURES
    keys = parts * part_tokens
    tile = pl.BlockSpec((GROUP * BLOCK, width), lambda i: (i, 0))
    next_tile = pl.BlockSpec(
        (BLOCK, width), lambda i: (jnp.minimum((i + 1) * GROUP, blocks - 1), 0)
    )

    def whole(value):
        return pl.BlockSpec(value.shape, lambda i: (0,) * value.ndim)

    def group_of(array, start, _):
        return pl.BlockSpec((GROUP,) + array.shape[1:], lambda i: (start // GROUP + i, 0, 0))

    def one_of(array, _, at):
        return pl.BlockSpec((1,) + array.shape[1:], lambda i: (at, 0, 0))

    def kv_scratch(group):
        return pltpu.VMEM((parts, group, part_tokens, 2 * width), jnp.bfloat16)

    out = jax.ShapeDtypeStruct((tokens, width), jnp.bfloat16)
    return pl.pallas_call(
        functools.partial(main_kernel, len(pieces)),
        grid=(blocks // GROUP,),
        out_shape=(out, out),
        in_specs=[pl.BlockSpec(memory_space=pltpu.SMEM), tile, next_tile, tile, next_tile]
        + [group_of(*piece) for piece in pieces]
        + [one_of(*piece) for piece in pieces]
        + [whole(h) for h in held],
        out_specs=(tile, tile),
        scratch_shapes=[
            pltpu.VMEM((FEATURES, 2 * width), jnp.bfloat16),
            kv_scratch(GROUP),
            kv_scratch(1),
            pltpu.VMEM((2, BLOCK, width), jnp.float32),
        ],
        compiler_params=pltpu.CompilerParams(vmem_limit_bytes=56 * 1024 * 1024),
        cost_estimate=pl.CostEstimate(
            flops=2 * (blocks + 1) * keys * 2 * width * (FEATURES + 2 * BLOCK),
            bytes_accessed=2 * (blocks * keys * FEATURES + 4 * tokens * width),
            transcendentals=blocks * keys * BLOCK * width // DH,
        ),
        name="blocks",
    )(place, queries, queries, grads, grads, *arrays, *arrays, *held)


def body(queries, context_grad, database, neighbour_ids, owner_map, key_weight, value_weight):
    seq_count = lax.axis_size("seq")
    head_devices = lax.axis_size("head")
    y_count = seq_count // Z
    local_rows, neigh_tokens, enc_width = database.shape
    part_tokens = neigh_tokens // head_devices
    my_head = lax.axis_index("head")

    request_ids = neighbour_ids.reshape(-1)
    row_labels = jnp.arange(owner_map.shape[0], dtype=jnp.int32)
    stored = jnp.sum(
        jnp.where(request_ids[:, None] == row_labels[None, :], owner_map[None, :], 0),
        axis=1,
        dtype=jnp.int32,
    )
    owner_index = stored // local_rows
    local_row = stored % local_rows
    slot_labels = jnp.arange(seq_count, dtype=jnp.int32)
    asked_rows = jnp.sum(
        jnp.where(owner_index[:, None] == slot_labels[None, :], local_row[:, None], 0),
        axis=0,
        dtype=jnp.int32,
    )
    asked_rows, key_weight = lax.optimization_barrier((asked_rows, key_weight))
    wanted = lax.all_to_all(
        asked_rows.reshape(seq_count, 1), "seq", split_axis=0, concat_axis=0, tiled=True
    ).reshape(-1)

    def moved(value, y_steps, z_flip):
        pairs = [
            (i, (i // Z + y_steps) % y_count * Z + (i % Z ^ z_flip)) for i in range(seq_count)
        ]
        return lax.ppermute(value, "seq", pairs)

    weight = jnp.concatenate([key_weight, value_weight], axis=1)[None]
    for step in (8, 4):
        weight = jnp.concatenate([weight, moved(weight, 0, step)], axis=0)

    parts = database.reshape(local_rows, head_devices, part_tokens, enc_width)
    mine = lax.dynamic_index_in_dim(parts, my_head, axis=1, keepdims=False)
    wanted, weight = lax.optimization_barrier((wanted, weight))
    outgoing = mine[wanted]
    weight = jnp.concatenate([weight, moved(weight, 0, 2)], axis=0)
    outgoing, weight = lax.optimization_barrier((outgoing, weight))
    incoming = lax.all_to_all(outgoing, "seq", split_axis=0, concat_axis=0, tiled=True)
    held = [moved(weight, k // 2, k % 2) for k in range(1, 2 * y_count)]
    asked = incoming[owner_index]
    asked, held = lax.optimization_barrier((asked, [weight, *held]))
    asked = jnp.concatenate([asked, shifted(asked[-2:], "seq", 1)], axis=0)

    def along_x(value, steps):
        return lax.ppermute(
            value, "head", [(i, (i + 2 * steps) % head_devices) for i in range(head_devices)]
        )

    def other_core(value):
        return lax.ppermute(value, "head", [(i, i ^ 1) for i in range(head_devices)])

    half = enc_width // 2
    def together(came, own):
        return jnp.concatenate([came[:-2], own[:-2], came[-2:], own[-2:]], axis=0)

    low, high = asked[:, :, :half], asked[:, :, half:]
    before_low, after_high = along_x(low, 1), along_x(high, -1)
    up, down = along_x(together(before_low, high), 1), along_x(together(after_high, low), -1)
    near = [asked, before_low, after_high]
    swapped = [other_core(a) for a in near]
    up, down, swapped = lax.optimization_barrier((up, down, swapped))
    blocks = queries.shape[0] // BLOCK
    pieces = []
    for arrays in (near + [up, down], swapped + [other_core(up), other_core(down)]):
        arrays = [a.reshape(-1, 2 * part_tokens, a.shape[-1]) for a in arrays]
        asked, before_low, after_high, up, down = arrays
        pieces += [(asked, 0, blocks)]
        pieces += [(before_low, 0, blocks), (up, blocks, 2 * blocks + 1)]
        pieces += [(down, blocks, 2 * blocks + 1), (after_high, 0, blocks)]
        pieces += [(up, 0, 2 * blocks), (down, 0, 2 * blocks)]

    my_seq = lax.axis_index("seq")
    place = jnp.stack([my_seq // Z, my_seq % Z]).astype(jnp.int32)
    return attention(place, queries, context_grad, pieces, held)


def solution(mesh):
    return jax.shard_map(
        body,
        mesh=mesh,
        in_specs=(
            P("seq", "head"),
            P("seq", "head"),
            P("seq", None, None),
            P("seq", None),
            P(),
            P("seq", "head"),
            P("seq", "head"),
        ),
        out_specs=(P("seq", "head"), P("seq", "head")),
        check_vma=False,
    )
```

```python
import functools

import jax
import jax.numpy as jnp
from jax import lax
from jax.experimental import pallas as pl
from jax.experimental.pallas import tpu as pltpu
from jax.sharding import PartitionSpec as P

DH = 128
BLOCK = 64
FEATURES = 1024
Z = 16
GROUP = 4


def shifted(value, axis, steps):
    count = lax.axis_size(axis)
    first, last = (max(0, -steps), min(count, count - steps))
    return lax.ppermute(value, axis, [(source, source + steps) for source in range(first, last)])


def scores_of(left, right):
    last = (((1,), (1,)), ((), ()))
    return lax.dot_general(left, right, last, preferred_element_type=jnp.float32)


def grouped(refs):
    groups = []
    for ref in refs:
        if groups and groups[-1][0].shape[-1] < FEATURES and len(groups[-1]) == 1:
            groups[-1].append(ref)
        else:
            groups.append([ref])
    return groups


def project(piece_refs, weight_ref, kv_ref):
    rows = []
    for group in grouped(piece_refs):
        parts = [ref[...].reshape(-1, ref.shape[-1]) for ref in group]
        rows.append(parts[0] if len(parts) == 1 else jnp.concatenate(parts, axis=1))
    kv = jnp.dot(
        jnp.concatenate(rows, axis=0), weight_ref[...], preferred_element_type=jnp.float32
    )
    kv_ref[...] = kv.astype(jnp.bfloat16).reshape(kv_ref.shape)


def attend(queries, grads, kv_ref):
    scale = DH ** (-0.5)
    width = queries[0].shape[1]
    pairs = [(at, head) for at in range(len(queries)) for head in range(width // DH)]
    keys, values, scores, prob_grad = [], [], [], []
    for at, head in pairs:
        own = slice(head * DH, (head + 1) * DH)
        other = slice(width + head * DH, width + (head + 1) * DH)
        keys.append(kv_ref[:, at, :, own].reshape(-1, DH))
        values.append(kv_ref[:, at, :, other].reshape(-1, DH))
        scores.append(scores_of(queries[at][:, own], keys[-1]))
        prob_grad.append(scores_of(grads[at][:, own], values[-1]))
    scores = jnp.concatenate(scores, axis=0) * scale
    prob_grad = jnp.concatenate(prob_grad, axis=0)
    weights = jnp.exp(scores - jnp.max(scores, axis=-1, keepdims=True))
    probabilities = weights / jnp.sum(weights, axis=-1, keepdims=True)
    delta = jnp.sum(probabilities * prob_grad, axis=-1, keepdims=True)
    probs_low = probabilities.astype(jnp.bfloat16)
    dscore = (probabilities * (prob_grad - delta) * scale).astype(jnp.bfloat16)
    blocks = [([], []) for _ in queries]
    for i, (at, head) in enumerate(pairs):
        rows = slice(i * BLOCK, (i + 1) * BLOCK)
        blocks[at][0].append(jnp.dot(probs_low[rows], values[i], preferred_element_type=jnp.float32))
        blocks[at][1].append(jnp.dot(dscore[rows], keys[i], preferred_element_type=jnp.float32))
    return [tuple(jnp.concatenate(heads, axis=1) for heads in block) for block in blocks]


def block_rows(ref, next_ref, at, count, last_row):
    here = ref[at * BLOCK : (at + 1) * BLOCK, :]
    there = next_ref[...] if at + 1 == count else ref[(at + 1) * BLOCK : (at + 2) * BLOCK, :]
    rows = jnp.where(last_row, here.astype(jnp.float32), there.astype(jnp.float32))
    return rows.astype(jnp.bfloat16)


def main_kernel(pieces_count, place_ref, query_ref, next_query_ref, grad_ref, next_grad_ref, *refs):
    piece_refs, refs = refs[:pieces_count], refs[pieces_count:]
    before_refs, refs = refs[:pieces_count], refs[pieces_count:]
    *held_refs, context_ref, qgrad_ref, weight_ref, kv_ref, before_kv_ref, carry_ref = refs

    @pl.when(pl.program_id(0) == 0)
    def _():
        rows = held_refs[0].shape[1]
        for step, held_ref in enumerate(held_refs):
            y = lax.rem(place_ref[0] + len(held_refs) - step, len(held_refs))
            for m in range(Z):
                at = (m & 3) * 4 + (m >> 2 & 1) * 2 + (m >> 3)
                start = (y * Z + (place_ref[1] ^ m)) * rows
                weight_ref[pl.ds(pl.multiple_of(start, 16), rows), :] = held_ref[at]
        project(before_refs, weight_ref, before_kv_ref)
        ((context, qgrad),) = attend([query_ref[:BLOCK, :]], [grad_ref[:BLOCK, :]], before_kv_ref)
        carry_ref[0] = context
        carry_ref[1] = qgrad

    project(piece_refs, weight_ref, kv_ref)
    count = kv_ref.shape[1]
    row = lax.broadcasted_iota(jnp.int32, (BLOCK, query_ref.shape[1]), 0)
    last_row = row == BLOCK - 1
    queries = [block_rows(query_ref, next_query_ref, at, count, last_row) for at in range(count)]
    grads = [block_rows(grad_ref, next_grad_ref, at, count, last_row) for at in range(count)]
    before = carry_ref[0], carry_ref[1]
    for at, now in enumerate(attend(queries, grads, kv_ref)):
        for out_ref, old, new in zip((context_ref, qgrad_ref), before, now):
            tile = jnp.where(last_row, new, old)
            out_ref[at * BLOCK : (at + 1) * BLOCK, :] = tile.astype(jnp.bfloat16)
        before = now
    carry_ref[0], carry_ref[1] = before


def attention(place, queries, grads, pieces, held):
    tokens, width = queries.shape
    blocks = tokens // BLOCK
    arrays = [array for array, _, _ in pieces]
    part_tokens = arrays[0].shape[1]
    parts = sum(a.shape[-1] for a in arrays) // FEATURES
    keys = parts * part_tokens
    tile = pl.BlockSpec((GROUP * BLOCK, width), lambda i: (i, 0))
    next_tile = pl.BlockSpec(
        (BLOCK, width), lambda i: (jnp.minimum((i + 1) * GROUP, blocks - 1), 0)
    )

    def whole(value):
        return pl.BlockSpec(value.shape, lambda i: (0,) * value.ndim)

    def group_of(array, start, _):
        return pl.BlockSpec((GROUP,) + array.shape[1:], lambda i: (start // GROUP + i, 0, 0))

    def one_of(array, _, at):
        return pl.BlockSpec((1,) + array.shape[1:], lambda i: (at, 0, 0))

    def kv_scratch(group):
        return pltpu.VMEM((parts, group, part_tokens, 2 * width), jnp.bfloat16)

    out = jax.ShapeDtypeStruct((tokens, width), jnp.bfloat16)
    return pl.pallas_call(
        functools.partial(main_kernel, len(pieces)),
        grid=(blocks // GROUP,),
        out_shape=(out, out),
        in_specs=[pl.BlockSpec(memory_space=pltpu.SMEM), tile, next_tile, tile, next_tile]
        + [group_of(*piece) for piece in pieces]
        + [one_of(*piece) for piece in pieces]
        + [whole(h) for h in held],
        out_specs=(tile, tile),
        scratch_shapes=[
            pltpu.VMEM((FEATURES, 2 * width), jnp.bfloat16),
            kv_scratch(GROUP),
            kv_scratch(1),
            pltpu.VMEM((2, BLOCK, width), jnp.float32),
        ],
        compiler_params=pltpu.CompilerParams(vmem_limit_bytes=56 * 1024 * 1024),
        cost_estimate=pl.CostEstimate(
            flops=2 * (blocks + 1) * keys * 2 * width * (FEATURES + 2 * BLOCK),
            bytes_accessed=2 * (blocks * keys * FEATURES + 4 * tokens * width),
            transcendentals=blocks * keys * BLOCK * width // DH,
        ),
        name="blocks",
    )(place, queries, queries, grads, grads, *arrays, *arrays, *held)


def body(queries, context_grad, database, neighbour_ids, owner_map, key_weight, value_weight):
    seq_count = lax.axis_size("seq")
    head_devices = lax.axis_size("head")
    y_count = seq_count // Z
    local_rows, neigh_tokens, enc_width = database.shape
    part_tokens = neigh_tokens // head_devices
    my_head = lax.axis_index("head")

    request_ids = neighbour_ids.reshape(-1)
    row_labels = jnp.arange(owner_map.shape[0], dtype=jnp.int32)
    stored = jnp.sum(
        jnp.where(request_ids[:, None] == row_labels[None, :], owner_map[None, :], 0),
        axis=1,
        dtype=jnp.int32,
    )
    owner_index = stored // local_rows
    local_row = stored % local_rows
    slot_labels = jnp.arange(seq_count, dtype=jnp.int32)
    asked_rows = jnp.sum(
        jnp.where(owner_index[:, None] == slot_labels[None, :], local_row[:, None], 0),
        axis=0,
        dtype=jnp.int32,
    )
    asked_rows, key_weight = lax.optimization_barrier((asked_rows, key_weight))
    wanted = lax.all_to_all(
        asked_rows.reshape(seq_count, 1), "seq", split_axis=0, concat_axis=0, tiled=True
    ).reshape(-1)

    def from_z(value, step):
        return lax.ppermute(value, "seq", [(i, i ^ step) for i in range(seq_count)])

    weight = jnp.concatenate([key_weight, value_weight], axis=1)[None]
    for step in (8, 4):
        weight = jnp.concatenate([weight, from_z(weight, step)], axis=0)

    parts = database.reshape(local_rows, head_devices, part_tokens, enc_width)
    mine = lax.dynamic_index_in_dim(parts, my_head, axis=1, keepdims=False)
    wanted, weight = lax.optimization_barrier((wanted, weight))
    outgoing = mine[wanted]
    outgoing, weight = lax.optimization_barrier((outgoing, weight))
    incoming = lax.all_to_all(outgoing, "seq", split_axis=0, concat_axis=0, tiled=True)
    weight = jnp.concatenate([weight] + [from_z(weight, step) for step in (1, 2, 3)], axis=0)
    asked = incoming[owner_index]
    weight, asked = lax.optimization_barrier((weight, asked))
    asked = jnp.concatenate([asked, shifted(asked[-2:], "seq", 1)], axis=0)

    def along_x(value, steps):
        return lax.ppermute(
            value, "head", [(i, (i + 2 * steps) % head_devices) for i in range(head_devices)]
        )

    def other_core(value):
        return lax.ppermute(value, "head", [(i, i ^ 1) for i in range(head_devices)])

    half = enc_width // 2
    def together(came, own):
        return jnp.concatenate([came[:-2], own[:-2], came[-2:], own[-2:]], axis=0)

    low, high = asked[:, :, :half], asked[:, :, half:]
    before_low, after_high = along_x(low, 1), along_x(high, -1)
    swapped, before_low, after_high = lax.optimization_barrier(
        (other_core(asked), before_low, after_high)
    )
    up, down = along_x(together(before_low, high), 1), along_x(together(after_high, low), -1)
    held = []
    for step in range(1, y_count):
        pairs = [(i, (i + step * Z) % seq_count) for i in range(seq_count)]
        held.append(lax.ppermute(weight, "seq", pairs))
    swapped_half = other_core(together(before_low, after_high))
    up, down, swapped_half, held = lax.optimization_barrier((up, down, swapped_half, held))
    held = [weight, *held]
    blocks = queries.shape[0] // BLOCK
    alone, first_of, second_of = (0, blocks), (0, 2 * blocks), (blocks, 2 * blocks + 1)

    def placed(array, where):
        return (array.reshape(-1, 2 * part_tokens, array.shape[-1]), *where)

    swapped_up, swapped_down = other_core(up), other_core(down)
    pieces = [
        placed(asked, alone),
        placed(before_low, alone),
        placed(up, second_of),
        placed(down, second_of),
        placed(after_high, alone),
        placed(up, first_of),
        placed(down, first_of),
        placed(swapped, alone),
        placed(swapped_half, first_of),
        placed(swapped_up, second_of),
        placed(swapped_down, second_of),
        placed(swapped_half, second_of),
        placed(swapped_up, first_of),
        placed(swapped_down, first_of),
    ]
    my_seq = lax.axis_index("seq")
    place = jnp.stack([my_seq // Z, my_seq % Z]).astype(jnp.int32)
    return attention(place, queries, context_grad, pieces, held)


def solution(mesh):
    return jax.shard_map(
        body,
        mesh=mesh,
        in_specs=(
            P("seq", "head"),
            P("seq", "head"),
            P("seq", None, None),
            P("seq", None),
            P(),
            P("seq", "head"),
            P("seq", "head"),
        ),
        out_specs=(P("seq", "head"), P("seq", "head")),
        check_vma=False,
    )
```

```python
import functools

import jax
import jax.numpy as jnp
from jax import lax
from jax.experimental import pallas as pl
from jax.experimental.pallas import tpu as pltpu
from jax.sharding import PartitionSpec as P

DH = 128
BLOCK = 64
FEATURES = 1024
SHARED = 640
Z = 16
GROUP = 4


def shifted(value, axis, steps):
    count = lax.axis_size(axis)
    first, last = (max(0, -steps), min(count, count - steps))
    return lax.ppermute(value, axis, [(source, source + steps) for source in range(first, last)])


def scores_of(left, right):
    last = (((1,), (1,)), ((), ()))
    return lax.dot_general(left, right, last, preferred_element_type=jnp.float32)


def grouped(refs):
    groups = []
    for ref in refs:
        if groups and sum(r.shape[-1] for r in groups[-1]) < FEATURES - SHARED:
            groups[-1].append(ref)
        else:
            groups.append([ref])
    return groups


def project(head, shared_ref, piece_refs, weight_ref, kv_ref):
    count = shared_ref.shape[0]
    rows = []
    for at, group in enumerate(grouped(piece_refs)):
        steps = (0, -1, 1, 2)[at % 4]
        source = lax.rem(head + 2 * steps + count, count) ^ (at // 4)
        parts = [shared_ref[source]] + [ref[...] for ref in group]
        parts = [part.reshape(-1, part.shape[-1]) for part in parts]
        rows.append(jnp.concatenate(parts, axis=1))
    kv = jnp.dot(
        jnp.concatenate(rows, axis=0), weight_ref[...], preferred_element_type=jnp.float32
    )
    kv_ref[...] = kv.astype(jnp.bfloat16).reshape(kv_ref.shape)


def attend(queries, grads, kv_ref):
    scale = DH ** (-0.5)
    width = queries[0].shape[1]
    pairs = [(at, head) for at in range(len(queries)) for head in range(width // DH)]
    keys, values, scores, prob_grad = [], [], [], []
    for at, head in pairs:
        own = slice(head * DH, (head + 1) * DH)
        other = slice(width + head * DH, width + (head + 1) * DH)
        keys.append(kv_ref[:, at, :, own].reshape(-1, DH))
        values.append(kv_ref[:, at, :, other].reshape(-1, DH))
        scores.append(scores_of(queries[at][:, own], keys[-1]))
        prob_grad.append(scores_of(grads[at][:, own], values[-1]))
    scores = jnp.concatenate(scores, axis=0) * scale
    prob_grad = jnp.concatenate(prob_grad, axis=0)
    weights = jnp.exp(scores - jnp.max(scores, axis=-1, keepdims=True))
    probabilities = weights / jnp.sum(weights, axis=-1, keepdims=True)
    delta = jnp.sum(probabilities * prob_grad, axis=-1, keepdims=True)
    probs_low = probabilities.astype(jnp.bfloat16)
    dscore = (probabilities * (prob_grad - delta) * scale).astype(jnp.bfloat16)
    blocks = [([], []) for _ in queries]
    for i, (at, head) in enumerate(pairs):
        rows = slice(i * BLOCK, (i + 1) * BLOCK)
        blocks[at][0].append(jnp.dot(probs_low[rows], values[i], preferred_element_type=jnp.float32))
        blocks[at][1].append(jnp.dot(dscore[rows], keys[i], preferred_element_type=jnp.float32))
    return [tuple(jnp.concatenate(heads, axis=1) for heads in block) for block in blocks]


def block_rows(ref, next_ref, at, count, last_row):
    here = ref[at * BLOCK : (at + 1) * BLOCK, :]
    there = next_ref[...] if at + 1 == count else ref[(at + 1) * BLOCK : (at + 2) * BLOCK, :]
    rows = jnp.where(last_row, here.astype(jnp.float32), there.astype(jnp.float32))
    return rows.astype(jnp.bfloat16)


def main_kernel(pieces_count, place_ref, query_ref, next_query_ref, grad_ref, next_grad_ref, *refs):
    shared_ref, before_shared_ref, *refs = refs
    head = place_ref[2]
    piece_refs, refs = refs[:pieces_count], refs[pieces_count:]
    before_refs, refs = refs[:pieces_count], refs[pieces_count:]
    *held_refs, context_ref, qgrad_ref, weight_ref, kv_ref, before_kv_ref, carry_ref = refs

    @pl.when(pl.program_id(0) == 0)
    def _():
        rows = held_refs[0].shape[1]
        for step, held_ref in enumerate(held_refs):
            y = lax.rem(place_ref[0] + len(held_refs) - step, len(held_refs))
            for m in range(Z):
                at = (m & 3) * 4 + (m >> 2 & 1) * 2 + (m >> 3)
                start = (y * Z + (place_ref[1] ^ m)) * rows
                weight_ref[pl.ds(pl.multiple_of(start, 16), rows), :] = held_ref[at]
        project(head, before_shared_ref, before_refs, weight_ref, before_kv_ref)
        ((context, qgrad),) = attend([query_ref[:BLOCK, :]], [grad_ref[:BLOCK, :]], before_kv_ref)
        carry_ref[0] = context
        carry_ref[1] = qgrad

    project(head, shared_ref, piece_refs, weight_ref, kv_ref)
    count = kv_ref.shape[1]
    row = lax.broadcasted_iota(jnp.int32, (BLOCK, query_ref.shape[1]), 0)
    last_row = row == BLOCK - 1
    queries = [block_rows(query_ref, next_query_ref, at, count, last_row) for at in range(count)]
    grads = [block_rows(grad_ref, next_grad_ref, at, count, last_row) for at in range(count)]
    before = carry_ref[0], carry_ref[1]
    for at, now in enumerate(attend(queries, grads, kv_ref)):
        for out_ref, old, new in zip((context_ref, qgrad_ref), before, now):
            tile = jnp.where(last_row, new, old)
            out_ref[at * BLOCK : (at + 1) * BLOCK, :] = tile.astype(jnp.bfloat16)
        before = now
    carry_ref[0], carry_ref[1] = before


def attention(place, queries, grads, shared, pieces, held):
    tokens, width = queries.shape
    blocks = tokens // BLOCK
    part_tokens = pieces[0].shape[1]
    parts = shared.shape[0]
    keys = parts * part_tokens
    tile = pl.BlockSpec((GROUP * BLOCK, width), lambda i: (i, 0))
    next_tile = pl.BlockSpec(
        (BLOCK, width), lambda i: (jnp.minimum((i + 1) * GROUP, blocks - 1), 0)
    )

    def whole(value):
        return pl.BlockSpec(value.shape, lambda i: (0,) * value.ndim)

    def kv_scratch(group):
        return pltpu.VMEM((parts, group, part_tokens, 2 * width), jnp.bfloat16)

    out = jax.ShapeDtypeStruct((tokens, width), jnp.bfloat16)
    return pl.pallas_call(
        functools.partial(main_kernel, len(pieces)),
        grid=(blocks // GROUP,),
        out_shape=(out, out),
        in_specs=[pl.BlockSpec(memory_space=pltpu.SMEM), tile, next_tile, tile, next_tile]
        + [
            pl.BlockSpec((parts, GROUP, part_tokens, SHARED), lambda i: (0, i, 0, 0)),
            pl.BlockSpec((parts, 1, part_tokens, SHARED), lambda i: (0, blocks, 0, 0)),
        ]
        + [pl.BlockSpec((GROUP,) + p.shape[1:], lambda i: (i, 0, 0)) for p in pieces]
        + [pl.BlockSpec((1,) + p.shape[1:], lambda i: (blocks, 0, 0)) for p in pieces]
        + [whole(h) for h in held],
        out_specs=(tile, tile),
        scratch_shapes=[
            pltpu.VMEM((FEATURES, 2 * width), jnp.bfloat16),
            kv_scratch(GROUP),
            kv_scratch(1),
            pltpu.VMEM((2, BLOCK, width), jnp.float32),
        ],
        compiler_params=pltpu.CompilerParams(vmem_limit_bytes=56 * 1024 * 1024),
        cost_estimate=pl.CostEstimate(
            flops=2 * (blocks + 1) * keys * 2 * width * (FEATURES + 2 * BLOCK),
            bytes_accessed=2 * (blocks * keys * FEATURES + 4 * tokens * width),
            transcendentals=blocks * keys * BLOCK * width // DH,
        ),
        name="blocks",
    )(
        place, queries, queries, grads, grads, shared, shared, *pieces, *pieces, *held
    )


def body(queries, context_grad, database, neighbour_ids, owner_map, key_weight, value_weight):
    seq_count = lax.axis_size("seq")
    head_devices = lax.axis_size("head")
    y_count = seq_count // Z
    local_rows, neigh_tokens, enc_width = database.shape
    part_tokens = neigh_tokens // head_devices
    my_head = lax.axis_index("head")

    request_ids = neighbour_ids.reshape(-1)
    row_labels = jnp.arange(owner_map.shape[0], dtype=jnp.int32)
    stored = jnp.sum(
        jnp.where(request_ids[:, None] == row_labels[None, :], owner_map[None, :], 0),
        axis=1,
        dtype=jnp.int32,
    )
    owner_index = stored // local_rows
    local_row = stored % local_rows
    slot_labels = jnp.arange(seq_count, dtype=jnp.int32)
    asked_rows = jnp.sum(
        jnp.where(owner_index[:, None] == slot_labels[None, :], local_row[:, None], 0),
        axis=0,
        dtype=jnp.int32,
    )
    asked_rows, key_weight = lax.optimization_barrier((asked_rows, key_weight))
    wanted = lax.all_to_all(
        asked_rows.reshape(seq_count, 1), "seq", split_axis=0, concat_axis=0, tiled=True
    ).reshape(-1)

    def from_z(value, step):
        return lax.ppermute(value, "seq", [(i, i ^ step) for i in range(seq_count)])

    weight = jnp.concatenate([key_weight, value_weight], axis=1)[None]
    for step in (8, 4):
        weight = jnp.concatenate([weight, from_z(weight, step)], axis=0)

    parts = database.reshape(local_rows, head_devices, part_tokens, enc_width)
    mine = lax.dynamic_index_in_dim(parts, my_head, axis=1, keepdims=False)
    wanted, weight = lax.optimization_barrier((wanted, weight))
    outgoing = mine[wanted]
    outgoing, weight = lax.optimization_barrier((outgoing, weight))
    incoming = lax.all_to_all(outgoing, "seq", split_axis=0, concat_axis=0, tiled=True)
    weight = jnp.concatenate([weight] + [from_z(weight, step) for step in (1, 2, 3)], axis=0)
    asked = incoming[owner_index]
    weight, asked = lax.optimization_barrier((weight, asked))
    asked = jnp.concatenate([asked, shifted(asked[-2:], "seq", 1)], axis=0)

    def along_x(value, steps):
        return lax.ppermute(
            value, "head", [(i, (i + 2 * steps) % head_devices) for i in range(head_devices)]
        )

    def other_core(value):
        return lax.ppermute(value, "head", [(i, i ^ 1) for i in range(head_devices)])

    shared = lax.all_gather(asked[:, :, :SHARED], "head", axis=0, tiled=False)
    shared = shared.reshape(head_devices, -1, 2 * part_tokens, SHARED)
    asked = asked[:, :, SHARED:]
    before, after = along_x(asked, 1), along_x(asked, -1)
    across = along_x(before[:, :, :DH], 1), along_x(after[:, :, DH:], -1)
    pieces = [asked, before, after, *across]
    pieces += [other_core(piece) for piece in pieces]
    pieces = [piece.reshape(-1, 2 * part_tokens, piece.shape[-1]) for piece in pieces]

    held = [weight]
    for step in range(1, y_count):
        pairs = [(i, (i + step * Z) % seq_count) for i in range(seq_count)]
        held.append(lax.ppermute(weight, "seq", pairs))
    my_seq = lax.axis_index("seq")
    place = jnp.stack([my_seq // Z, my_seq % Z, my_head]).astype(jnp.int32)
    return attention(place, queries, context_grad, shared, pieces, held)


def solution(mesh):
    return jax.shard_map(
        body,
        mesh=mesh,
        in_specs=(
            P("seq", "head"),
            P("seq", "head"),
            P("seq", None, None),
            P("seq", None),
            P(),
            P("seq", "head"),
            P("seq", "head"),
        ),
        out_specs=(P("seq", "head"), P("seq", "head")),
        check_vma=False,
    )
```

```python
import functools

import jax
import jax.numpy as jnp
from jax import lax
from jax.experimental import pallas as pl
from jax.experimental.pallas import tpu as pltpu
from jax.sharding import PartitionSpec as P

DH = 128
BLOCK = 64
FEATURES = 1024
Z = 16
GROUP = 4


def shifted(value, axis, steps):
    count = lax.axis_size(axis)
    first, last = (max(0, -steps), min(count, count - steps))
    return lax.ppermute(value, axis, [(source, source + steps) for source in range(first, last)])


def scores_of(left, right):
    last = (((1,), (1,)), ((), ()))
    return lax.dot_general(left, right, last, preferred_element_type=jnp.float32)


def grouped(refs):
    groups = []
    for ref in refs:
        if groups and groups[-1][0].shape[-1] < FEATURES and len(groups[-1]) == 1:
            groups[-1].append(ref)
        else:
            groups.append([ref])
    return groups


def project(piece_refs, weight_ref, kv_ref):
    rows = []
    for group in grouped(piece_refs):
        parts = [ref[...].reshape(-1, ref.shape[-1]) for ref in group]
        rows.append(parts[0] if len(parts) == 1 else jnp.concatenate(parts, axis=1))
    kv = jnp.dot(
        jnp.concatenate(rows, axis=0), weight_ref[...], preferred_element_type=jnp.float32
    )
    kv_ref[...] = kv.astype(jnp.bfloat16).reshape(kv_ref.shape)


def attend(queries, grads, kv_ref):
    scale = DH ** (-0.5)
    width = queries[0].shape[1]
    pairs = [(at, head) for at in range(len(queries)) for head in range(width // DH)]
    keys, values, scores, prob_grad = [], [], [], []
    for at, head in pairs:
        own = slice(head * DH, (head + 1) * DH)
        other = slice(width + head * DH, width + (head + 1) * DH)
        keys.append(kv_ref[:, at, :, own].reshape(-1, DH))
        values.append(kv_ref[:, at, :, other].reshape(-1, DH))
        scores.append(scores_of(queries[at][:, own], keys[-1]))
        prob_grad.append(scores_of(grads[at][:, own], values[-1]))
    scores = jnp.concatenate(scores, axis=0) * scale
    prob_grad = jnp.concatenate(prob_grad, axis=0)
    weights = jnp.exp(scores - jnp.max(scores, axis=-1, keepdims=True))
    probabilities = weights / jnp.sum(weights, axis=-1, keepdims=True)
    delta = jnp.sum(probabilities * prob_grad, axis=-1, keepdims=True)
    probs_low = probabilities.astype(jnp.bfloat16)
    dscore = (probabilities * (prob_grad - delta) * scale).astype(jnp.bfloat16)
    blocks = [([], []) for _ in queries]
    for i, (at, head) in enumerate(pairs):
        rows = slice(i * BLOCK, (i + 1) * BLOCK)
        blocks[at][0].append(jnp.dot(probs_low[rows], values[i], preferred_element_type=jnp.float32))
        blocks[at][1].append(jnp.dot(dscore[rows], keys[i], preferred_element_type=jnp.float32))
    return [tuple(jnp.concatenate(heads, axis=1) for heads in block) for block in blocks]


def block_rows(ref, next_ref, at, count, last_row):
    here = ref[at * BLOCK : (at + 1) * BLOCK, :]
    there = next_ref[...] if at + 1 == count else ref[(at + 1) * BLOCK : (at + 2) * BLOCK, :]
    rows = jnp.where(last_row, here.astype(jnp.float32), there.astype(jnp.float32))
    return rows.astype(jnp.bfloat16)


def main_kernel(pieces_count, place_ref, query_ref, next_query_ref, grad_ref, next_grad_ref, *refs):
    piece_refs, refs = refs[:pieces_count], refs[pieces_count:]
    before_refs, refs = refs[:pieces_count], refs[pieces_count:]
    *held_refs, context_ref, qgrad_ref, weight_ref, kv_ref, before_kv_ref, carry_ref = refs

    @pl.when(pl.program_id(0) == 0)
    def _():
        rows = held_refs[0].shape[1]
        y_count = len(held_refs) // 2
        for k, held_ref in enumerate(held_refs):
            y = lax.rem(place_ref[0] + y_count - k // 2, y_count)
            for at in range(held_ref.shape[0]):
                m = (at & 1) * 8 + (at >> 1 & 1) * 4 + (at >> 2) * 2 + k % 2
                start = (y * Z + (place_ref[1] ^ m)) * rows
                weight_ref[pl.ds(pl.multiple_of(start, 16), rows), :] = held_ref[at]
        project(before_refs, weight_ref, before_kv_ref)
        ((context, qgrad),) = attend([query_ref[:BLOCK, :]], [grad_ref[:BLOCK, :]], before_kv_ref)
        carry_ref[0] = context
        carry_ref[1] = qgrad

    project(piece_refs, weight_ref, kv_ref)
    count = kv_ref.shape[1]
    row = lax.broadcasted_iota(jnp.int32, (BLOCK, query_ref.shape[1]), 0)
    last_row = row == BLOCK - 1
    queries = [block_rows(query_ref, next_query_ref, at, count, last_row) for at in range(count)]
    grads = [block_rows(grad_ref, next_grad_ref, at, count, last_row) for at in range(count)]
    before = carry_ref[0], carry_ref[1]
    for at, now in enumerate(attend(queries, grads, kv_ref)):
        for out_ref, old, new in zip((context_ref, qgrad_ref), before, now):
            tile = jnp.where(last_row, new, old)
            out_ref[at * BLOCK : (at + 1) * BLOCK, :] = tile.astype(jnp.bfloat16)
        before = now
    carry_ref[0], carry_ref[1] = before


def attention(place, queries, grads, pieces, held):
    tokens, width = queries.shape
    blocks = tokens // BLOCK
    arrays = [array for array, _, _ in pieces]
    part_tokens = arrays[0].shape[1]
    parts = sum(a.shape[-1] for a in arrays) // FEATURES
    keys = parts * part_tokens
    tile = pl.BlockSpec((GROUP * BLOCK, width), lambda i: (i, 0))
    next_tile = pl.BlockSpec(
        (BLOCK, width), lambda i: (jnp.minimum((i + 1) * GROUP, blocks - 1), 0)
    )

    def whole(value):
        return pl.BlockSpec(value.shape, lambda i: (0,) * value.ndim)

    def group_of(array, start, _):
        return pl.BlockSpec((GROUP,) + array.shape[1:], lambda i: (start // GROUP + i, 0, 0))

    def one_of(array, _, at):
        return pl.BlockSpec((1,) + array.shape[1:], lambda i: (at, 0, 0))

    def kv_scratch(group):
        return pltpu.VMEM((parts, group, part_tokens, 2 * width), jnp.bfloat16)

    out = jax.ShapeDtypeStruct((tokens, width), jnp.bfloat16)
    return pl.pallas_call(
        functools.partial(main_kernel, len(pieces)),
        grid=(blocks // GROUP,),
        out_shape=(out, out),
        in_specs=[pl.BlockSpec(memory_space=pltpu.SMEM), tile, next_tile, tile, next_tile]
        + [group_of(*piece) for piece in pieces]
        + [one_of(*piece) for piece in pieces]
        + [whole(h) for h in held],
        out_specs=(tile, tile),
        scratch_shapes=[
            pltpu.VMEM((FEATURES, 2 * width), jnp.bfloat16),
            kv_scratch(GROUP),
            kv_scratch(1),
            pltpu.VMEM((2, BLOCK, width), jnp.float32),
        ],
        compiler_params=pltpu.CompilerParams(vmem_limit_bytes=56 * 1024 * 1024),
        cost_estimate=pl.CostEstimate(
            flops=2 * (blocks + 1) * keys * 2 * width * (FEATURES + 2 * BLOCK),
            bytes_accessed=2 * (blocks * keys * FEATURES + 4 * tokens * width),
            transcendentals=blocks * keys * BLOCK * width // DH,
        ),
        name="blocks",
    )(place, queries, queries, grads, grads, *arrays, *arrays, *held)


def body(queries, context_grad, database, neighbour_ids, owner_map, key_weight, value_weight):
    seq_count = lax.axis_size("seq")
    head_devices = lax.axis_size("head")
    y_count = seq_count // Z
    local_rows, neigh_tokens, enc_width = database.shape
    part_tokens = neigh_tokens // head_devices
    my_head = lax.axis_index("head")

    request_ids = neighbour_ids.reshape(-1)
    row_labels = jnp.arange(owner_map.shape[0], dtype=jnp.int32)
    stored = jnp.sum(
        jnp.where(request_ids[:, None] == row_labels[None, :], owner_map[None, :], 0),
        axis=1,
        dtype=jnp.int32,
    )
    owner_index = stored // local_rows
    local_row = stored % local_rows
    slot_labels = jnp.arange(seq_count, dtype=jnp.int32)
    asked_rows = jnp.sum(
        jnp.where(owner_index[:, None] == slot_labels[None, :], local_row[:, None], 0),
        axis=0,
        dtype=jnp.int32,
    )
    asked_rows, key_weight = lax.optimization_barrier((asked_rows, key_weight))
    wanted = lax.all_to_all(
        asked_rows.reshape(seq_count, 1), "seq", split_axis=0, concat_axis=0, tiled=True
    ).reshape(-1)

    def moved(value, y_steps, z_flip):
        pairs = [
            (i, (i // Z + y_steps) % y_count * Z + (i % Z ^ z_flip)) for i in range(seq_count)
        ]
        return lax.ppermute(value, "seq", pairs)

    weight = jnp.concatenate([key_weight, value_weight], axis=1)[None]
    for step in (8, 4):
        weight = jnp.concatenate([weight, moved(weight, 0, step)], axis=0)

    parts = database.reshape(local_rows, head_devices, part_tokens, enc_width)
    mine = lax.dynamic_index_in_dim(parts, my_head, axis=1, keepdims=False)
    wanted, weight = lax.optimization_barrier((wanted, weight))
    outgoing = mine[wanted]
    weight = jnp.concatenate([weight, moved(weight, 0, 2)], axis=0)
    outgoing, weight = lax.optimization_barrier((outgoing, weight))
    incoming = lax.all_to_all(outgoing, "seq", split_axis=0, concat_axis=0, tiled=True)
    late = (2, 2 * y_count - 2)
    held = {k: moved(weight, k // 2, k % 2) for k in range(1, 2 * y_count) if k not in late}
    asked = incoming[owner_index]
    asked, weight, held = lax.optimization_barrier((asked, weight, held))
    asked = jnp.concatenate([asked, shifted(asked[-2:], "seq", 1)], axis=0)

    def along_x(value, steps):
        return lax.ppermute(
            value, "head", [(i, (i + 2 * steps) % head_devices) for i in range(head_devices)]
        )

    def other_core(value):
        return lax.ppermute(value, "head", [(i, i ^ 1) for i in range(head_devices)])

    half = enc_width // 2
    def together(came, own):
        return jnp.concatenate([came[:-2], own[:-2], came[-2:], own[-2:]], axis=0)

    low, high = asked[:, :, :half], asked[:, :, half:]
    before_low, after_high = along_x(low, 1), along_x(high, -1)
    up, down = along_x(together(before_low, high), 1), along_x(together(after_high, low), -1)
    near = [asked, before_low, after_high]
    swapped = [other_core(a) for a in near]
    rest = {k: moved(weight, k // 2, k % 2) for k in late}
    up, down, swapped, rest = lax.optimization_barrier((up, down, swapped, rest))
    held = {0: weight, **held, **rest}
    held = [held[k] for k in range(2 * y_count)]
    blocks = queries.shape[0] // BLOCK
    pieces = []
    for arrays in (near + [up, down], swapped + [other_core(up), other_core(down)]):
        arrays = [a.reshape(-1, 2 * part_tokens, a.shape[-1]) for a in arrays]
        asked, before_low, after_high, up, down = arrays
        pieces += [(asked, 0, blocks)]
        pieces += [(before_low, 0, blocks), (up, blocks, 2 * blocks + 1)]
        pieces += [(down, blocks, 2 * blocks + 1), (after_high, 0, blocks)]
        pieces += [(up, 0, 2 * blocks), (down, 0, 2 * blocks)]

    my_seq = lax.axis_index("seq")
    place = jnp.stack([my_seq // Z, my_seq % Z]).astype(jnp.int32)
    return attention(place, queries, context_grad, pieces, held)


def solution(mesh):
    return jax.shard_map(
        body,
        mesh=mesh,
        in_specs=(
            P("seq", "head"),
            P("seq", "head"),
            P("seq", None, None),
            P("seq", None),
            P(),
            P("seq", "head"),
            P("seq", "head"),
        ),
        out_specs=(P("seq", "head"), P("seq", "head")),
        check_vma=False,
    )
```
